512 devices in a mesh: dp: 64 (over x, z), mp: 8 (over y, core).
Axes of the slice: x: 4, y: 4, z: 16, core: 2. Of those that a mesh axis runs over, the one named last changes fastest.
Arguments:
- activations: bfloat16 [16384, 512], P('dp'), may hold values from -6 to 6
- cotangent: bfloat16 [16384, 24576], P('dp', 'mp'), may hold values from -0.375 to 0.375
- block_scale: bfloat16 [32768, 192], P('dp', 'mp'), may hold values from 0.0009994507 to 0.049804688
- master_weight: float32 [512, 24576], P('dp', 'mp'), may hold values from -6 to 6
- moment_one: float32 [512, 24576], P('dp', 'mp'), may hold values from -4 to 4
- moment_two: float32 [512, 24576], P('dp', 'mp'), may hold values from 0.05 to 2
Outputs:
- new_weight: bfloat16 [512, 24576], P('dp')
- master_out: float32 [512, 24576], P('dp', 'mp')
- moment_one_out: float32 [512, 24576], P('dp', 'mp')
- moment_two_out: float32 [512, 24576], P('dp', 'mp')
The draws below stay inside these ranges and needn't reach their ends.
All inputs are finite; a program needn't handle non-finite values.
Results may differ from the reference program's by a relative error of at most 0.0026.
Values may be sent and summed in bfloat16 or wider, within the bound.
A program may use at most 64 MiB of HBM per device.

```python
import math
import jax
import jax.numpy as jnp
from jax import lax

FF = 24576
BUCKET = 512
TOK_DEV = 256
TOKENS = 16384
N_DP = 64


def steps_of(stream_key, dims, split, smallest, largest):
    factor_of, own = 1.0, jax.random.fold_in(stream_key, 6)
    for dim, shards_of in split:
        heights = jnp.exp(jax.random.uniform(jax.random.fold_in(own, dim), (shards_of,), jnp.float32, smallest / len(split), largest / len(split)))
        factor_of = factor_of * jnp.repeat(heights, dims[dim] // shards_of).reshape([-1 if axis == dim else 1 for axis in range(len(dims))])
    return factor_of


def centred(stream_key, extent, width, reach, cuts=(), kind=jnp.bfloat16):
    factor_of = steps_of(stream_key, extent, cuts, -0.22, 0.18) if cuts else 1.0
    entries = jax.random.normal(stream_key, extent, jnp.float32) * width * factor_of
    return jnp.minimum(jnp.maximum(entries, -reach), reach).astype(kind)


def setup_inputs(seed: int = 0) -> dict:
    splits = jax.random.split(jax.random.key(seed), 7)
    return {
        "activations": centred(splits[0], (TOKENS, BUCKET), 1.0, 6.0, ((0, 64),)),
        "cotangent": centred(splits[1], (TOKENS, FF), TOK_DEV ** -0.5, 0.375, ((0, 64), (1, 8))),
        "block_scale": jnp.clip(jnp.exp(math.log(0.049804688) - 3.9086586 * jax.random.uniform(splits[2], (N_DP * BUCKET, FF // 128), jnp.float32) ** steps_of(splits[2], (N_DP * BUCKET, FF // 128), ((0, 64), (1, 8)), -0.2, 0.2)), 0.0009994507, 0.049804688).astype(jnp.bfloat16),
        "master_weight": centred(splits[3], (BUCKET, FF), 1.0, 6.0, ((0, 64), (1, 8)), jnp.float32),
        "moment_one": centred(splits[4], (BUCKET, FF), 0.3, 4.0, ((0, 64), (1, 8)), jnp.float32),
        "moment_two": jnp.clip(jnp.exp(math.log(2.0) - 3.6888794 * jax.random.uniform(splits[5], (BUCKET, FF), jnp.float32) ** steps_of(splits[5], (BUCKET, FF), ((0, 64), (1, 8)), -0.2, 0.2)), 0.05, 2.0),
    }


bias_one = 0.9999734386011124
bias_two = 0.994079470779666

def hadamard_table():
    indices = jnp.arange(128, dtype=jnp.int32)
    anded = jnp.bitwise_and(indices[:, None], indices[None, :])
    parity = jnp.zeros((128, 128), jnp.int32)
    for shift in range(7):
        parity = parity + jnp.bitwise_and(jnp.right_shift(anded, shift), 1)
    signs = 1 - 2 * jnp.bitwise_and(parity, 1)
    return signs.astype(jnp.float32) / jnp.sqrt(jnp.float32(128.0))

def rotate(matrix, table):
    row_count, col_count = matrix.shape
    blocks = matrix.reshape(row_count, col_count // 128, 128)
    turned = jnp.einsum('rbk,kj->rbj', blocks, table, precision=lax.Precision.HIGHEST)
    return turned.reshape(row_count, col_count)

def quantize(matrix, scales, table):
    row_count, col_count = matrix.shape
    blocks = rotate(matrix, table).reshape(row_count, col_count // 128, 128)
    scaled = blocks / scales.astype(jnp.float32)[:, :, None]
    quant = jnp.clip(scaled, -448.0, 448.0).astype(jnp.bfloat16)
    return quant

def reference(activations, cotangent, block_scale, master_weight, moment_one, moment_two):
    table = hadamard_table()
    act_groups = activations.reshape(N_DP, TOK_DEV, BUCKET)
    cot_groups = cotangent.reshape(N_DP, TOK_DEV, FF)
    scale_groups = block_scale.reshape(N_DP, BUCKET, FF // 128)

    def accumulate(total, triple):
        partial_grad = lax.dot_general(triple[0], triple[1], (((0,), (0,)), ((), ())), preferred_element_type=jnp.float32)
        quant = quantize(partial_grad, triple[2], table)
        restored = quant.astype(jnp.float32) * triple[2].astype(jnp.float32)[:, :, None]
        return (total + restored.reshape(BUCKET, FF), None)
    total, unused = lax.scan(accumulate, jnp.zeros((BUCKET, FF), jnp.float32), (act_groups, cot_groups, scale_groups))
    gradient = rotate(total, table)
    moment_one_out = 0.9 * moment_one + 0.1 * gradient
    moment_two_out = 0.95 * moment_two + 0.05 * gradient * gradient
    first_hat = moment_one_out / bias_one
    second_hat = moment_two_out / bias_two
    master_out = master_weight - 0.01 * (first_hat / (jnp.sqrt(second_hat) + 1e-08) + 0.1 * master_weight)
    return (master_out.astype(jnp.bfloat16), master_out, moment_one_out, moment_two_out)
```

```python
import functools
import math

import jax
import jax.numpy as jnp
from jax import lax
from jax.experimental import pallas as pl
from jax.experimental.pallas import tpu as pltpu
from jax.sharding import PartitionSpec as P

BIAS_ONE = 0.9999734386011124
BIAS_TWO = 0.994079470779666
NX, NZ, NMP = 4, 16, 8
ROWS = 8
COLS = 3072
BLOCKS = COLS // 128
CHUNKS = 4
W = COLS // CHUNKS
TILE = 256
HALF = NZ // 2
UNIT = 2.0**20
ROOT = 1.0 / math.sqrt(128.0)
F32, BF16 = jnp.float32, jnp.bfloat16


def encode(x):
    return ((x * jnp.abs(x)) * (x * x)).astype(BF16)


def decode(y):
    y = y.astype(F32)
    size = jnp.maximum(jnp.abs(y), 2.0**-124)
    r = lax.rsqrt(size)
    return y * (r * lax.rsqrt(size * r))


def split(x, parts):
    out = []
    for _ in range(parts):
        piece = x.astype(BF16)
        out.append(piece)
        x = x - piece.astype(F32)
    return out


def signs(size):
    i = lax.broadcasted_iota(jnp.int32, (size, size), 0)
    j = lax.broadcasted_iota(jnp.int32, (size, size), 1)
    both = i & j
    odd = both & 1
    for bit in range(1, 7):
        odd = odd ^ ((both >> bit) & 1)
    same = (i >> 7) == (j >> 7)
    return jnp.where(same, (1 - 2 * odd).astype(F32), 0.0).astype(BF16)


def dot(a, b):
    return lax.dot_general(a, b, (((1,), (0,)), ((), ())), preferred_element_type=F32)


def kernel(
    act_ref, cot_ref, scale_ref, master_ref, one_ref, two_ref,
    weight_out, master_out, one_out, two_out,
    act_t, scale_t, table, values, ring_out, ring_in, x_out, x_in, w_out, w_in,
    ring_ss, ring_rs, x_ss, x_rs, w_ss, w_rs,
):
    dp, mp = lax.axis_index("dp"), lax.axis_index("mp")
    x, z = dp // NZ, lax.rem(dp, NZ)

    def at_z(step):
        return {"dp": x * NZ + lax.rem(z + step + NZ, NZ)}

    def at_x(step):
        return {"dp": lax.rem(x + step + NX, NX) * NZ + z}

    def at_mp(step):
        return {"mp": lax.rem(mp + step + NMP, NMP)}

    barrier = pltpu.get_barrier_semaphore()
    partners = [at_z(1), at_z(-1)]
    partners += [at_x(j) for j in range(1, NX)] + [at_mp(j) for j in range(1, NMP)]
    for partner in partners:
        pl.semaphore_signal(barrier, inc=1, device_id=partner)

    act_t[...] = act_ref[...].astype(F32).T.astype(BF16)
    scale = scale_ref[...].astype(F32)
    parts = [p.astype(F32) for p in split(ROOT / scale, 3)]
    pad = jnp.zeros((128 - 4 * BLOCKS, NX * NZ * ROWS), F32)
    scale_t[...] = jnp.concatenate([scale] + parts + [pad], axis=0).T.astype(BF16)
    table[...] = signs(TILE)

    def local_tile(tile):
        cols = pl.ds(pl.multiple_of(tile * TILE, TILE), TILE)
        turned = split(dot(cot_ref[:, cols], table[...]), 2)
        k = lax.broadcasted_iota(jnp.int32, (128, 2 * TILE), 0)
        n = lax.broadcasted_iota(jnp.int32, (128, 2 * TILE), 1)
        block = tile * (TILE // 128) + ((n >> 7) & (TILE // 128 - 1))
        in_scale = jnp.where(k == block, UNIT, 0.0)
        hit = (k == block + BLOCKS) | (k == block + 2 * BLOCKS) | (k == block + 3 * BLOCKS)
        pick = jnp.where(n < TILE, in_scale, jnp.where(hit, 1.0, 0.0)).astype(BF16)
        for part in range(NX):
            rows = slice(part * NZ * ROWS, (part + 1) * NZ * ROWS)
            a = act_t[rows, :]
            grad = dot(a, turned[0]) + dot(a, turned[1])
            both = dot(scale_t[rows, :], pick)
            quant = jnp.clip(grad * both[:, TILE:], -448.0, 448.0).astype(BF16)
            values[part, :, :, cols] = (quant.astype(F32) * both[:, :TILE]).reshape(NZ, ROWS, TILE)

    def ring_copy(c, d, s, width=W):
        return pltpu.make_async_remote_copy(
            src_ref=ring_out.at[c, d, s, :, pl.ds(0, width)],
            dst_ref=ring_in.at[c, d, s, :, pl.ds(0, width)],
            send_sem=ring_ss.at[c, d, s],
            recv_sem=ring_rs.at[c, d, s],
            device_id=at_z(1 - 2 * d),
        )

    def own(c, zd, lo):
        return values[:, zd, :, c * W + lo : c * W + lo + 128].reshape(NX * ROWS, 128)

    def target(d, s):
        return lax.rem(z + (1 - 2 * d) * (HALF - s) + NZ, NZ)

    def first(c):
        for d in range(2):
            zd = target(d, 0)
            for lo in range(0, W // 2, 128):
                ring_out[c, d, 0, :, lo : lo + 128] = encode(own(c, zd, lo + d * (W // 2)))
            ring_copy(c, d, 0, W // 2).start()

    def pass_on(c, d, s, half):
        zd = target(d, s)
        ring_copy(c, d, s - 1, W // 2 if half else W).wait_recv()
        for lo in range(0, W, 128):
            total = own(c, zd, lo)
            if not half:
                total = total + decode(ring_in[c, d, s - 1, :, lo : lo + 128])
            elif lo // (W // 2) == d:
                at = lo - d * (W // 2)
                total = total + decode(ring_in[c, d, 0, :, at : at + 128])
            ring_out[c, d, s, :, lo : lo + 128] = encode(total)
        ring_copy(c, d, s).start()

    def x_copy(c, j):
        return pltpu.make_async_remote_copy(
            src_ref=x_out.at[c, lax.rem(x + j, NX)],
            dst_ref=x_in.at[c, j - 1],
            send_sem=x_ss.at[c, j - 1],
            recv_sem=x_rs.at[c, j - 1],
            device_id=at_x(j),
        )

    def w_copy(c, j, slot):
        return pltpu.make_async_remote_copy(
            src_ref=w_out.at[c],
            dst_ref=w_in.at[c, slot],
            send_sem=w_ss.at[c, j - 1],
            recv_sem=w_rs.at[c, slot],
            device_id=at_mp(j),
        )

    per = W // TILE
    for c in range(CHUNKS):
        lax.fori_loop(c * per, (c + 1) * per, lambda t, _: (local_tile(t), 0)[1], 0)
        if c == 0:
            pl.semaphore_wait(barrier, len(partners))
        first(c)
    for c in range(CHUNKS):
        for d in range(2):
            pass_on(c, d, 1, True)

    def step(s, carry):
        for c in range(CHUNKS):
            for d in range(2):
                pass_on(c, d, s, False)
        return carry

    lax.fori_loop(2, HALF, step, 0)

    for c in range(CHUNKS):
        for d in range(2):
            ring_copy(c, d, HALF - 1).wait_recv()
        for lo in range(0, W, 128):
            total = own(c, z, lo) + decode(ring_in[c, 0, HALF - 1, :, lo : lo + 128])
            total = total + decode(ring_in[c, 1, HALF - 1, :, lo : lo + 128])
            x_out[c, :, :, lo : lo + 128] = total.reshape(NX, ROWS, 128)
        for j in range(1, NX):
            x_copy(c, j).start()

    for c in range(CHUNKS):
        for j in range(1, NX):
            x_copy(c, j).wait_recv()
        total = x_out[c, x]
        for j in range(1, NX):
            total = total + x_in[c, j - 1]
        stack = jnp.concatenate([total[:, lo : lo + 128] for lo in range(0, W, 128)], axis=0)
        pieces = split(stack, 3)
        turned = dot(pieces[0], table[:128, :128])
        turned = turned + dot(pieces[1], table[:128, :128])
        turned = (turned + dot(pieces[2], table[:128, :128])) * (ROOT / UNIT)
        blocks = []
        for b in range(W // 128):
            cols = slice(c * W + b * 128, c * W + (b + 1) * 128)
            gradient = turned[b * ROWS : (b + 1) * ROWS, :]
            one = 0.9 * one_ref[:, cols] + 0.1 * gradient
            two = 0.95 * two_ref[:, cols] + 0.05 * gradient * gradient
            master = master_ref[:, cols]
            change = (one / BIAS_ONE) / (jnp.sqrt(two / BIAS_TWO) + 1e-08)
            master = master - 0.01 * (change + 0.1 * master)
            one_out[:, cols] = one
            two_out[:, cols] = two
            master_out[:, cols] = master
            blocks.append(master)
        for b in range(W // 256):
            pair = jnp.concatenate([blocks[b], blocks[b + W // 256]], axis=0).astype(BF16)
            w_out[c, :, b * 128 : (b + 1) * 128] = pair
        for j in range(1, NMP):
            w_copy(c, j, mp).start()

    for c in range(CHUNKS):
        w_in[c, mp] = w_out[c]
        for j in range(1, NMP):
            w_copy(c, j, lax.rem(mp - j + NMP, NMP)).wait_recv()
        for source in range(NMP):
            both = w_in[c, source].astype(F32)
            at = source * COLS + c * W
            weight_out[:, at : at + W // 2] = both[:ROWS].astype(BF16)
            weight_out[:, at + W // 2 : at + W] = both[ROWS:].astype(BF16)

    for c in range(CHUNKS):
        for d in range(2):
            ring_copy(c, d, 0, W // 2).wait_send()
            lax.fori_loop(1, HALF, lambda s, _: (ring_copy(c, d, s).wait_send(), 0)[1], 0)
        for j in range(1, NX):
            x_copy(c, j).wait_send()
        for j in range(1, NMP):
            w_copy(c, j, mp).wait_send()


def local(activations, cotangent, block_scale, master_weight, moment_one, moment_two):
    vmem = pl.BlockSpec(memory_space=pltpu.VMEM)
    rows = NX * NZ * ROWS
    state = jax.ShapeDtypeStruct((ROWS, COLS), F32)
    dma = pltpu.SemaphoreType.DMA
    return pl.pallas_call(
        kernel,
        out_shape=(jax.ShapeDtypeStruct((ROWS, COLS * NMP), BF16), state, state, state),
        in_specs=[vmem] * 6,
        out_specs=(vmem,) * 4,
        scratch_shapes=[
            pltpu.VMEM((rows, 256), BF16),
            pltpu.VMEM((rows, 128), BF16),
            pltpu.VMEM((TILE, TILE), BF16),
            pltpu.VMEM((NX, NZ, ROWS, COLS), F32),
            pltpu.VMEM((CHUNKS, 2, HALF, NX * ROWS, W), BF16),
            pltpu.VMEM((CHUNKS, 2, HALF, NX * ROWS, W), BF16),
            pltpu.VMEM((CHUNKS, NX, ROWS, W), F32),
            pltpu.VMEM((CHUNKS, NX - 1, ROWS, W), F32),
            pltpu.VMEM((CHUNKS, 2 * ROWS, W // 2), BF16),
            pltpu.VMEM((CHUNKS, NMP, 2 * ROWS, W // 2), BF16),
            dma((CHUNKS, 2, HALF)),
            dma((CHUNKS, 2, HALF)),
            dma((CHUNKS, NX - 1)),
            dma((CHUNKS, NX - 1)),
            dma((CHUNKS, NMP - 1)),
            dma((CHUNKS, NMP)),
        ],
        compiler_params=pltpu.CompilerParams(
            collective_id=0, has_side_effects=True, vmem_limit_bytes=48 * 2**20
        ),
        cost_estimate=pl.CostEstimate(flops=3 * 10**9, bytes_accessed=4 * 10**6, transcendentals=0),
    )(activations, cotangent, block_scale.T, master_weight, moment_one, moment_two)


def solution(mesh):
    return jax.shard_map(
        local,
        mesh=mesh,
        in_specs=(P("dp", None),) + (P("dp", "mp"),) * 5,
        out_specs=(P("dp", None),) + (P("dp", "mp"),) * 3,
        check_vma=False,
    )
```

```python
import functools
import math

import jax
import jax.numpy as jnp
from jax import lax
from jax.experimental import pallas as pl
from jax.experimental.pallas import tpu as pltpu
from jax.sharding import PartitionSpec as P

BIAS_ONE = 0.9999734386011124
BIAS_TWO = 0.994079470779666
NX, NZ, NMP = 4, 16, 8
ROWS = 8
GROUP = NX * ROWS
COLS = 3072
BLOCKS = COLS // 128
CHUNKS = 4
W = COLS // CHUNKS
TILE = 256
HALF = NZ // 2
UNIT = 2.0**20
ROOT = 1.0 / math.sqrt(128.0)
F32, BF16 = jnp.float32, jnp.bfloat16


def encode(x):
    return ((x * jnp.abs(x)) * (x * x)).astype(BF16)


def decode(y):
    y = y.astype(F32)
    size = jnp.maximum(jnp.abs(y), 2.0**-124)
    r = lax.rsqrt(size)
    return y * (r * lax.rsqrt(size * r))


def split(x, parts):
    out = []
    for _ in range(parts):
        piece = x.astype(BF16)
        out.append(piece)
        x = x - piece.astype(F32)
    return out


def signs(size):
    i = lax.broadcasted_iota(jnp.int32, (size, size), 0)
    j = lax.broadcasted_iota(jnp.int32, (size, size), 1)
    both = i & j
    odd = both & 1
    for bit in range(1, 7):
        odd = odd ^ ((both >> bit) & 1)
    same = (i >> 7) == (j >> 7)
    return jnp.where(same, (1 - 2 * odd).astype(F32), 0.0).astype(BF16)


def dot(a, b):
    return lax.dot_general(a, b, (((1,), (0,)), ((), ())), preferred_element_type=F32)


def kernel(
    act_hbm, cot_hbm, scale_hbm, master_hbm, one_hbm, two_hbm,
    weight_out, master_out, one_out, two_out,
    act_ref, cot_ref, scale_ref, master_ref, one_ref, two_ref,
    act_t, scale_t, table, turned, values, ring_out, ring_in, x_out, x_in, w_out, w_in,
    load_sem, ring_ss, ring_rs, x_ss, x_rs, w_ss, w_rs,
):
    dp, mp = lax.axis_index("dp"), lax.axis_index("mp")
    x, z = dp // NZ, lax.rem(dp, NZ)

    def at_z(step):
        return {"dp": x * NZ + lax.rem(z + step + NZ, NZ)}

    def at_x(step):
        return {"dp": lax.rem(x + step + NX, NX) * NZ + z}

    def at_mp(step):
        return {"mp": lax.rem(mp + step + NMP, NMP)}

    barrier = pltpu.get_barrier_semaphore()
    partners = [at_z(1), at_z(-1)]
    partners += [at_x(j) for j in range(1, NX)] + [at_mp(j) for j in range(1, NMP)]
    for partner in partners:
        pl.semaphore_signal(barrier, inc=1, device_id=partner)

    loads = [(act_hbm, act_ref), (scale_hbm, scale_ref)]
    for c in range(CHUNKS):
        cols = slice(c * W, (c + 1) * W)
        loads.append((cot_hbm.at[:, cols], cot_ref.at[:, cols]))
    loads += [(one_hbm, one_ref), (two_hbm, two_ref), (master_hbm, master_ref)]
    loads = [pltpu.make_async_copy(s, d, load_sem.at[i]) for i, (s, d) in enumerate(loads)]
    for load in loads:
        load.start()

    table[...] = signs(TILE)
    loads[0].wait()
    act = act_ref[...].astype(F32).T
    for zd in range(NZ):
        rows = [act[(xd * NZ + zd) * ROWS : (xd * NZ + zd + 1) * ROWS] for xd in range(NX)]
        rows = jnp.concatenate(rows, axis=0).astype(BF16)
        act_t[zd * GROUP : (zd + 1) * GROUP, :] = jnp.concatenate([rows, rows], axis=1)
    loads[1].wait()
    scale = scale_ref[...].astype(F32)
    pad = jnp.ones((128 - BLOCKS, NX * NZ * ROWS), F32)
    scale = jnp.concatenate([scale, pad], axis=0).T
    for zd in range(NZ):
        for xd in range(NX):
            at = (xd * NZ + zd) * ROWS
            scale_t[zd * GROUP + xd * ROWS : zd * GROUP + (xd + 1) * ROWS, :] = scale[at : at + ROWS]
    for c in range(CHUNKS):
        loads[2 + c].wait()
        for lo in range(c * W, (c + 1) * W, TILE):
            high, low = split(dot(cot_ref[:, lo : lo + TILE], table[...]), 2)
            turned[:256, lo : lo + TILE] = high
            turned[256:, lo : lo + TILE] = low

    def local_rows(targets):
        spans = [pl.ds(pl.multiple_of(zd * GROUP, GROUP), GROUP) for zd in targets]
        rows = jnp.concatenate([act_t[span, :] for span in spans], axis=0)
        scales = jnp.concatenate([scale_t[span, :] for span in spans], axis=0)
        inverse = ROOT / scales
        for lo in range(0, COLS, TILE):
            grad = dot(rows, turned[:, lo : lo + TILE])
            for at in range(0, TILE, 128):
                b = (lo + at) // 128
                scaled = grad[:, at : at + 128] * inverse[:, b : b + 1]
                quant = jnp.clip(scaled, -448.0, 448.0).astype(BF16).astype(F32)
                value = quant * (scales[:, b : b + 1] * UNIT)
                for i, zd in enumerate(targets):
                    values[zd, :, lo + at : lo + at + 128] = value[i * GROUP : (i + 1) * GROUP]

    def ring_copy(c, d, s, width=W):
        return pltpu.make_async_remote_copy(
            src_ref=ring_out.at[c, d, s, :, pl.ds(0, width)],
            dst_ref=ring_in.at[c, d, s, :, pl.ds(0, width)],
            send_sem=ring_ss.at[c, d, s],
            recv_sem=ring_rs.at[c, d, s],
            device_id=at_z(1 - 2 * d),
        )

    def own(c, zd, lo):
        return values[zd, :, c * W + lo : c * W + lo + 128]

    def target(d, s):
        return lax.rem(z + (1 - 2 * d) * (HALF - s) + NZ, NZ)

    def first(c):
        zd = target(0, 0)
        for d in range(2):
            for lo in range(0, W // 2, 128):
                ring_out[c, d, 0, :, lo : lo + 128] = encode(own(c, zd, lo + d * (W // 2)))
            ring_copy(c, d, 0, W // 2).start()

    def pass_on(c, d, s, near=False):
        zd = target(d, s)
        begin, width = (d * (W // 2), W // 2) if near else (0, W)
        ring_copy(c, d, s - 1, width).wait_recv()
        for lo in range(0, W, 128):
            total = own(c, zd, lo)
            if begin <= lo < begin + width:
                at = lo - begin
                total = total + decode(ring_in[c, d, s - 1, :, at : at + 128])
            ring_out[c, d, s, :, lo : lo + 128] = encode(total)
        ring_copy(c, d, s).start()

    def x_copy(c, j):
        return pltpu.make_async_remote_copy(
            src_ref=x_out.at[c, lax.rem(x + j, NX)],
            dst_ref=x_in.at[c, j - 1],
            send_sem=x_ss.at[c, j - 1],
            recv_sem=x_rs.at[c, j - 1],
            device_id=at_x(j),
        )

    def w_copy(c, j, slot):
        return pltpu.make_async_remote_copy(
            src_ref=w_out.at[c],
            dst_ref=w_in.at[c, slot],
            send_sem=w_ss.at[c, j - 1],
            recv_sem=w_rs.at[c, slot],
            device_id=at_mp(j),
        )

    local_rows([target(0, 0)])
    pl.semaphore_wait(barrier, len(partners))
    for c in range(CHUNKS):
        first(c)
    local_rows([target(0, 1), target(1, 1)])
    for load in loads[-3:]:
        load.wait()

    def step(s, near=False):
        for c in range(CHUNKS):
            for d in range(2):
                pass_on(c, d, s, near)
        local_rows([target(0, s + 1), target(1, s + 1)])

    step(1, True)
    lax.fori_loop(2, HALF, lambda s, _: (step(s), 0)[1], 0)

    for c in range(CHUNKS):
        for d in range(2):
            ring_copy(c, d, HALF - 1).wait_recv()
        for lo in range(0, W, 128):
            total = own(c, z, lo) + decode(ring_in[c, 0, HALF - 1, :, lo : lo + 128])
            total = total + decode(ring_in[c, 1, HALF - 1, :, lo : lo + 128])
            x_out[c, :, :, lo : lo + 128] = total.reshape(NX, ROWS, 128)
        for j in (2, 1, 3):
            x_copy(c, j).start()

    for c in range(CHUNKS):
        for j in range(1, NX):
            x_copy(c, j).wait_recv()
        total = x_out[c, x]
        for j in range(1, NX):
            total = total + x_in[c, j - 1]
        stack = jnp.concatenate([total[:, lo : lo + 128] for lo in range(0, W, 128)], axis=0)
        pieces = split(stack, 3)
        back = dot(pieces[0], table[:128, :128])
        back = back + dot(pieces[1], table[:128, :128])
        back = (back + dot(pieces[2], table[:128, :128])) * (ROOT / UNIT)
        blocks = []
        for b in range(W // 128):
            cols = slice(c * W + b * 128, c * W + (b + 1) * 128)
            gradient = back[b * ROWS : (b + 1) * ROWS, :]
            one = 0.9 * one_ref[:, cols] + 0.1 * gradient
            two = 0.95 * two_ref[:, cols] + 0.05 * gradient * gradient
            master = master_ref[:, cols]
            change = (one / BIAS_ONE) / (jnp.sqrt(two / BIAS_TWO) + 1e-08)
            master = master - 0.01 * (change + 0.1 * master)
            one_out[:, cols] = one
            two_out[:, cols] = two
            master_out[:, cols] = master
            blocks.append(master)
        for b in range(W // 256):
            pair = jnp.concatenate([blocks[b], blocks[b + W // 256]], axis=0).astype(BF16)
            w_out[c, :, b * 128 : (b + 1) * 128] = pair
        for j in range(1, NMP):
            w_copy(c, j, mp).start()
        w_in[c, mp] = w_out[c]

    for c in range(CHUNKS):
        for j in range(1, NMP):
            w_copy(c, j, lax.rem(mp - j + NMP, NMP)).wait_recv()
        for source in range(NMP):
            both = w_in[c, source].astype(F32)
            at = source * COLS + c * W
            weight_out[:, at : at + W // 2] = both[:ROWS].astype(BF16)
            weight_out[:, at + W // 2 : at + W] = both[ROWS:].astype(BF16)

    for c in range(CHUNKS):
        for d in range(2):
            ring_copy(c, d, 0, W // 2).wait_send()
            lax.fori_loop(1, HALF, lambda s, _: (ring_copy(c, d, s).wait_send(), 0)[1], 0)
        for j in range(1, NX):
            x_copy(c, j).wait_send()
        for j in range(1, NMP):
            w_copy(c, j, mp).wait_send()


def write(*refs):
    sources, outs, sem = refs[:4], refs[4:8], refs[8]
    copies = [pltpu.make_async_copy(s, o, sem.at[i]) for i, (s, o) in enumerate(zip(sources, outs))]
    for copy in copies:
        copy.start()
    for copy in copies:
        copy.wait()


def local(activations, cotangent, block_scale, master_weight, moment_one, moment_two):
    vmem, hbm = pl.BlockSpec(memory_space=pltpu.VMEM), pl.BlockSpec(memory_space=pltpu.HBM)
    rows = NX * NZ * ROWS
    dma = pltpu.SemaphoreType.DMA
    args = (activations, cotangent, block_scale.T, master_weight, moment_one, moment_two)
    args = [pltpu.with_memory_space_constraint(arg, pltpu.HBM) for arg in args]
    shapes = (((ROWS, COLS * NMP), BF16),) + (((ROWS, COLS), F32),) * 3
    results = pl.pallas_call(
        kernel,
        out_shape=tuple(pltpu.VMEM(*shape) for shape in shapes),
        in_specs=[hbm] * 6,
        out_specs=(vmem,) * 4,
        scratch_shapes=[
            pltpu.VMEM((256, rows), BF16),
            pltpu.VMEM((256, COLS), BF16),
            pltpu.VMEM((BLOCKS, rows), BF16),
            pltpu.VMEM((ROWS, COLS), F32),
            pltpu.VMEM((ROWS, COLS), F32),
            pltpu.VMEM((ROWS, COLS), F32),
            pltpu.VMEM((rows, 512), BF16),
            pltpu.VMEM((rows, 128), F32),
            pltpu.VMEM((TILE, TILE), BF16),
            pltpu.VMEM((512, COLS), BF16),
            pltpu.VMEM((NZ, GROUP, COLS), F32),
            pltpu.VMEM((CHUNKS, 2, HALF, GROUP, W), BF16),
            pltpu.VMEM((CHUNKS, 2, HALF, GROUP, W), BF16),
            pltpu.VMEM((CHUNKS, NX, ROWS, W), F32),
            pltpu.VMEM((CHUNKS, NX - 1, ROWS, W), F32),
            pltpu.VMEM((CHUNKS, 2 * ROWS, W // 2), BF16),
            pltpu.VMEM((CHUNKS, NMP, 2 * ROWS, W // 2), BF16),
            dma((5 + CHUNKS,)),
            dma((CHUNKS, 2, HALF)),
            dma((CHUNKS, 2, HALF)),
            dma((CHUNKS, NX - 1)),
            dma((CHUNKS, NX - 1)),
            dma((CHUNKS, NMP - 1)),
            dma((CHUNKS, NMP)),
        ],
        compiler_params=pltpu.CompilerParams(
            collective_id=0, has_side_effects=True, vmem_limit_bytes=48 * 2**20
        ),
        cost_estimate=pl.CostEstimate(flops=3 * 10**9, bytes_accessed=4 * 10**6, transcendentals=0),
    )(*args)
    return pl.pallas_call(
        write,
        out_shape=tuple(jax.ShapeDtypeStruct(*shape) for shape in shapes),
        in_specs=[vmem] * 4,
        out_specs=(hbm,) * 4,
        scratch_shapes=[dma((4,))],
    )(*[pltpu.with_memory_space_constraint(r, pltpu.VMEM) for r in results])


def solution(mesh):
    return jax.shard_map(
        local,
        mesh=mesh,
        in_specs=(P("dp", None),) + (P("dp", "mp"),) * 5,
        out_specs=(P("dp", None),) + (P("dp", "mp"),) * 3,
        check_vma=False,
    )
```

```python
import functools
import math

import jax
import jax.numpy as jnp
from jax import lax
from jax.experimental import pallas as pl
from jax.experimental.pallas import tpu as pltpu
from jax.sharding import PartitionSpec as P

BIAS_ONE = 0.9999734386011124
BIAS_TWO = 0.994079470779666
NX, NZ, NMP = 4, 16, 8
ROWS = 8
GROUP = NX * ROWS
COLS = 3072
BLOCKS = COLS // 128
CHUNKS = 4
W = COLS // CHUNKS
SWAP = 2
WIDE = SWAP * W
FAR = WIDE // 2
TILE = 256
HALF = NZ // 2
UNIT = 2.0**20
ROOT = 1.0 / math.sqrt(128.0)
F32, BF16 = jnp.float32, jnp.bfloat16


def encode(x):
    return ((x * jnp.abs(x)) * (x * x)).astype(BF16)


def decode(y):
    y = y.astype(F32)
    size = jnp.maximum(jnp.abs(y), 2.0**-124)
    r = lax.rsqrt(size)
    return y * (r * lax.rsqrt(size * r))


def split(x, parts):
    out = []
    for _ in range(parts):
        piece = x.astype(BF16)
        out.append(piece)
        x = x - piece.astype(F32)
    return out


def signs(size):
    i = lax.broadcasted_iota(jnp.int32, (size, size), 0)
    j = lax.broadcasted_iota(jnp.int32, (size, size), 1)
    both = i & j
    odd = both & 1
    for bit in range(1, 7):
        odd = odd ^ ((both >> bit) & 1)
    same = (i >> 7) == (j >> 7)
    return jnp.where(same, (1 - 2 * odd).astype(F32), 0.0).astype(BF16)


def dot(a, b):
    return lax.dot_general(a, b, (((1,), (0,)), ((), ())), preferred_element_type=F32)


def kernel(
    act_hbm, cot_hbm, scale_hbm, master_hbm, one_hbm, two_hbm,
    weight_out, master_out, one_out, two_out,
    act_ref, cot_ref, scale_ref, master_ref, one_ref, two_ref,
    act_t, scale_t, table, turned, values, ring_out, ring_in, x_out, x_in, w_out, w_in,
    far_out, far_in, far_values, far_ring_out, far_ring_in,
    load_sem, ring_ss, ring_rs, x_ss, x_rs, w_ss, w_rs,
    far_ss, far_rs, far_ring_ss, far_ring_rs,
):
    dp, mp = lax.axis_index("dp"), lax.axis_index("mp")
    x, z = dp // NZ, lax.rem(dp, NZ)

    def at_z(step):
        return {"dp": x * NZ + lax.rem(z + step + NZ, NZ)}

    def at_x(step):
        return {"dp": lax.rem(x + step + NX, NX) * NZ + z}

    def at_mp(step):
        return {"mp": lax.rem(mp + step + NMP, NMP)}

    barrier = pltpu.get_barrier_semaphore()
    partners = [at_z(1), at_z(-1)]
    partners += [at_x(j) for j in range(1, NX)] + [at_mp(j) for j in range(1, NMP)]
    for partner in partners:
        pl.semaphore_signal(barrier, inc=1, device_id=partner)

    loads = [(act_hbm, act_ref), (scale_hbm, scale_ref)]
    near = range(SWAP, CHUNKS)
    for c in range(CHUNKS):
        cols = slice(c * W, (c + 1) * W)
        loads.append((cot_hbm.at[:, cols], cot_ref.at[:, cols]))
    loads += [(one_hbm, one_ref), (two_hbm, two_ref), (master_hbm, master_ref)]
    loads = [pltpu.make_async_copy(s, d, load_sem.at[i]) for i, (s, d) in enumerate(loads)]
    for load in loads:
        load.start()

    table[...] = signs(TILE)
    loads[0].wait()
    act = act_ref[...].astype(F32).T
    for zd in range(NZ):
        rows = [act[(xd * NZ + zd) * ROWS : (xd * NZ + zd + 1) * ROWS] for xd in range(NX)]
        rows = jnp.concatenate(rows, axis=0).astype(BF16)
        act_t[zd * GROUP : (zd + 1) * GROUP, :] = jnp.concatenate([rows, rows], axis=1)
    loads[1].wait()
    scale = scale_ref[...].astype(F32)
    pad = jnp.ones((128 - BLOCKS, NX * NZ * ROWS), F32)
    scale = jnp.concatenate([scale, pad], axis=0).T
    for zd in range(NZ):
        for xd in range(NX):
            at = (xd * NZ + zd) * ROWS
            scale_t[zd * GROUP + xd * ROWS : zd * GROUP + (xd + 1) * ROWS, :] = scale[at : at + ROWS]
    for c in range(CHUNKS):
        loads[2 + c].wait()
        for lo in range(c * W, (c + 1) * W, TILE):
            high, low = split(dot(cot_ref[:, lo : lo + TILE], table[...]), 2)
            turned[:256, lo : lo + TILE] = high
            turned[256:, lo : lo + TILE] = low

    def target(d, s):
        return lax.rem(z + (1 - 2 * d) * (HALF - s) + NZ, NZ)

    def pair(s):
        return (target(0, 0), z) if isinstance(s, int) and s == 0 else (target(0, s), target(1, s))

    def local_rows(s):
        targets = pair(s)
        spans = [pl.ds(pl.multiple_of(zd * GROUP, GROUP), GROUP) for zd in targets]
        rows = jnp.concatenate([act_t[span, :] for span in spans], axis=0)
        scales = jnp.concatenate([scale_t[span, :] for span in spans], axis=0)
        inverse = ROOT / scales
        for lo in range(0, COLS, TILE):
            grad = dot(rows, turned[:, lo : lo + TILE])
            for at in range(lo, lo + TILE, 128):
                b = at // 128
                scaled = grad[:, at - lo : at - lo + 128] * inverse[:, b : b + 1]
                quant = jnp.clip(scaled, -448.0, 448.0).astype(BF16).astype(F32)
                value = quant * (scales[:, b : b + 1] * UNIT)
                for i, zd in enumerate(targets):
                    values[zd, :, at : at + 128] = value[i * GROUP : (i + 1) * GROUP]
                if at < WIDE:
                    for xd in range(NX):
                        mine = [value[i * GROUP + xd * ROWS :][:ROWS] for i in range(2)]
                        far_out[s, xd, :, at : at + 128] = encode(jnp.concatenate(mine, axis=0))


    def far_copy(s, j):
        return pltpu.make_async_remote_copy(
            src_ref=far_out.at[s, lax.rem(x + j, NX)],
            dst_ref=far_in.at[s, j - 1],
            send_sem=far_ss.at[s, j - 1],
            recv_sem=far_rs.at[s, j - 1],
            device_id=at_x(j),
        )

    def far_send(s):
        for j in (2, 1, 3):
            far_copy(s, j).start()

    def far_sum(s):
        span = pl.ds(pl.multiple_of(x * ROWS, ROWS), ROWS)
        targets = pair(s)
        for j in range(1, NX):
            far_copy(s, j).wait_recv()
        for lo in range(0, WIDE, 128):
            cols = slice(lo, lo + 128)
            total = jnp.concatenate([values[zd, span, cols] for zd in targets], axis=0)
            for j in range(NX - 1):
                total = total + decode(far_in[s, j, :, cols])
            for i, zd in enumerate(targets):
                far_values[zd, :, cols] = total[i * ROWS : (i + 1) * ROWS]

    def far_ring_copy(d, s):
        return pltpu.make_async_remote_copy(
            src_ref=far_ring_out.at[d, s],
            dst_ref=far_ring_in.at[d, s],
            send_sem=far_ring_ss.at[d, s],
            recv_sem=far_ring_rs.at[d, s],
            device_id=at_z(1 - 2 * d),
        )

    def far_own(zd, lo):
        halves = [far_values[zd, :, at : at + 128] for at in (lo, FAR + lo)]
        return jnp.concatenate(halves, axis=0)

    def far_pass_on(d, s, fresh=False):
        zd = target(d, s)
        if not fresh:
            far_ring_copy(d, s - 1).wait_recv()
        for lo in range(0, FAR, 128):
            total = far_own(zd, lo)
            if not fresh:
                total = total + decode(far_ring_in[d, s - 1, :, lo : lo + 128])
            far_ring_out[d, s, :, lo : lo + 128] = encode(total)
        far_ring_copy(d, s).start()


    def ring_copy(c, d, s, width=W):
        return pltpu.make_async_remote_copy(
            src_ref=ring_out.at[c, d, s, :, pl.ds(0, width)],
            dst_ref=ring_in.at[c, d, s, :, pl.ds(0, width)],
            send_sem=ring_ss.at[c, d, s],
            recv_sem=ring_rs.at[c, d, s],
            device_id=at_z(1 - 2 * d),
        )

    def own(c, zd, lo):
        return values[zd, :, c * W + lo : c * W + lo + 128]

    def first(c):
        zd = target(0, 0)
        for d in range(2):
            for lo in range(0, W // 2, 128):
                ring_out[c, d, 0, :, lo : lo + 128] = encode(own(c, zd, lo + d * (W // 2)))
            ring_copy(c, d, 0, W // 2).start()

    def pass_on(c, d, s, near=False):
        zd = target(d, s)
        begin, width = (d * (W // 2), W // 2) if near else (0, W)
        ring_copy(c, d, s - 1, width).wait_recv()
        for lo in range(0, W, 128):
            total = own(c, zd, lo)
            if begin <= lo < begin + width:
                at = lo - begin
                total = total + decode(ring_in[c, d, s - 1, :, at : at + 128])
            ring_out[c, d, s, :, lo : lo + 128] = encode(total)
        ring_copy(c, d, s).start()

    def x_copy(c, j):
        return pltpu.make_async_remote_copy(
            src_ref=x_out.at[c, lax.rem(x + j, NX)],
            dst_ref=x_in.at[c, j - 1],
            send_sem=x_ss.at[c, j - 1],
            recv_sem=x_rs.at[c, j - 1],
            device_id=at_x(j),
        )

    def w_copy(c, j, slot):
        return pltpu.make_async_remote_copy(
            src_ref=w_out.at[c],
            dst_ref=w_in.at[c, slot],
            send_sem=w_ss.at[c, j - 1],
            recv_sem=w_rs.at[c, slot],
            device_id=at_mp(j),
        )

    def update(c, totals):
        pieces = split(jnp.concatenate(totals, axis=0), 3)
        back = dot(pieces[0], table[:128, :128])
        back = back + dot(pieces[1], table[:128, :128])
        back = (back + dot(pieces[2], table[:128, :128])) * (ROOT / UNIT)
        blocks = []
        for b in range(W // 128):
            cols = slice(c * W + b * 128, c * W + (b + 1) * 128)
            gradient = back[b * ROWS : (b + 1) * ROWS, :]
            one = 0.9 * one_ref[:, cols] + 0.1 * gradient
            two = 0.95 * two_ref[:, cols] + 0.05 * gradient * gradient
            master = master_ref[:, cols]
            change = (one / BIAS_ONE) / (jnp.sqrt(two / BIAS_TWO) + 1e-08)
            master = master - 0.01 * (change + 0.1 * master)
            one_out[:, cols] = one
            two_out[:, cols] = two
            master_out[:, cols] = master
            blocks.append(master)
        for b in range(W // 256):
            pair = jnp.concatenate([blocks[b], blocks[b + W // 256]], axis=0).astype(BF16)
            w_out[c, :, b * 128 : (b + 1) * 128] = pair
        for j in range(1, NMP):
            w_copy(c, j, mp).start()
        w_in[c, mp] = w_out[c]

    def gathered(c):
        for j in range(1, NMP):
            w_copy(c, j, lax.rem(mp - j + NMP, NMP)).wait_recv()
        for source in range(NMP):
            both = w_in[c, source].astype(F32)
            at = source * COLS + c * W
            weight_out[:, at : at + W // 2] = both[:ROWS].astype(BF16)
            weight_out[:, at + W // 2 : at + W] = both[ROWS:].astype(BF16)

    def far_step(s):
        far_sum(s)
        far_pass_on(0, s)
        far_pass_on(1, s)

    local_rows(0)
    pl.semaphore_wait(barrier, len(partners))
    for c in near:
        first(c)
    far_send(0)
    for s in (1, 2):
        local_rows(s)
        far_send(s)
    for load in loads[-3:]:
        load.wait()

    def near_step(s, edge=False):
        for c in near:
            for d in range(2):
                pass_on(c, d, s, edge)

    def ahead(s):
        local_rows(s + 2)
        far_send(s + 2)

    near_step(1, True)
    far_sum(0)
    far_pass_on(0, 0, True)
    ahead(1)
    near_step(2)
    far_sum(1)
    far_pass_on(0, 1)
    far_pass_on(1, 1, True)
    ahead(2)

    def step(s, carry):
        near_step(s)
        far_step(s - 1)
        ahead(s)
        return carry

    lax.fori_loop(3, HALF - 2, step, 0)
    for s in (HALF - 2, HALF - 1):
        near_step(s)
        far_step(s - 1)

    for c in near:
        for d in range(2):
            ring_copy(c, d, HALF - 1).wait_recv()
        for lo in range(0, W, 128):
            total = own(c, z, lo) + decode(ring_in[c, 0, HALF - 1, :, lo : lo + 128])
            total = total + decode(ring_in[c, 1, HALF - 1, :, lo : lo + 128])
            x_out[c, :, :, lo : lo + 128] = total.reshape(NX, ROWS, 128)
        for j in (2, 1, 3):
            x_copy(c, j).start()
    far_step(HALF - 1)

    for c in near:
        for j in range(1, NX):
            x_copy(c, j).wait_recv()
        total = x_out[c, x]
        for j in range(1, NX):
            total = total + x_in[c, j - 1]
        update(c, [total[:, lo : lo + 128] for lo in range(0, W, 128)])

    for d in range(2):
        far_ring_copy(d, HALF - 1).wait_recv()
    totals = []
    for lo in range(0, FAR, 128):
        total = far_own(z, lo) + decode(far_ring_in[0, HALF - 1, :, lo : lo + 128])
        totals.append(total + decode(far_ring_in[1, HALF - 1, :, lo : lo + 128]))
    totals = [t[:ROWS] for t in totals] + [t[ROWS:] for t in totals]
    for c in range(SWAP):
        update(c, totals[c * W // 128 : (c + 1) * W // 128])

    for c in (*near, *range(SWAP)):
        gathered(c)

    for j in range(1, NX):
        lax.fori_loop(0, HALF, lambda s, _: (far_copy(s, j).wait_send(), 0)[1], 0)
    for d in range(2):
        lax.fori_loop(d, HALF, lambda s, _: (far_ring_copy(d, s).wait_send(), 0)[1], 0)
    for c in near:
        for d in range(2):
            ring_copy(c, d, 0, W // 2).wait_send()
            lax.fori_loop(1, HALF, lambda s, _: (ring_copy(c, d, s).wait_send(), 0)[1], 0)
        for j in range(1, NX):
            x_copy(c, j).wait_send()
    for c in range(CHUNKS):
        for j in range(1, NMP):
            w_copy(c, j, mp).wait_send()


def write(*refs):
    sources, outs, sem = refs[:4], refs[4:8], refs[8]
    copies = [pltpu.make_async_copy(s, o, sem.at[i]) for i, (s, o) in enumerate(zip(sources, outs))]
    for copy in copies:
        copy.start()
    for copy in copies:
        copy.wait()


def local(activations, cotangent, block_scale, master_weight, moment_one, moment_two):
    vmem, hbm = pl.BlockSpec(memory_space=pltpu.VMEM), pl.BlockSpec(memory_space=pltpu.HBM)
    rows = NX * NZ * ROWS
    dma = pltpu.SemaphoreType.DMA
    args = (activations, cotangent, block_scale.T, master_weight, moment_one, moment_two)
    args = [pltpu.with_memory_space_constraint(arg, pltpu.HBM) for arg in args]
    shapes = (((ROWS, COLS * NMP), BF16),) + (((ROWS, COLS), F32),) * 3
    results = pl.pallas_call(
        kernel,
        out_shape=tuple(pltpu.VMEM(*shape) for shape in shapes),
        in_specs=[hbm] * 6,
        out_specs=(vmem,) * 4,
        scratch_shapes=[
            pltpu.VMEM((256, rows), BF16),
            pltpu.VMEM((256, COLS), BF16),
            pltpu.VMEM((BLOCKS, rows), BF16),
            pltpu.VMEM((ROWS, COLS), F32),
            pltpu.VMEM((ROWS, COLS), F32),
            pltpu.VMEM((ROWS, COLS), F32),
            pltpu.VMEM((rows, 512), BF16),
            pltpu.VMEM((rows, 128), F32),
            pltpu.VMEM((TILE, TILE), BF16),
            pltpu.VMEM((512, COLS), BF16),
            pltpu.VMEM((NZ, GROUP, COLS), F32),
            pltpu.VMEM((CHUNKS, 2, HALF, GROUP, W), BF16),
            pltpu.VMEM((CHUNKS, 2, HALF, GROUP, W), BF16),
            pltpu.VMEM((CHUNKS, NX, ROWS, W), F32),
            pltpu.VMEM((CHUNKS, NX - 1, ROWS, W), F32),
            pltpu.VMEM((CHUNKS, 2 * ROWS, W // 2), BF16),
            pltpu.VMEM((CHUNKS, NMP, 2 * ROWS, W // 2), BF16),
            pltpu.VMEM((HALF, NX, 2 * ROWS, WIDE), BF16),
            pltpu.VMEM((HALF, NX - 1, 2 * ROWS, WIDE), BF16),
            pltpu.VMEM((NZ, ROWS, WIDE), F32),
            pltpu.VMEM((2, HALF, 2 * ROWS, FAR), BF16),
            pltpu.VMEM((2, HALF, 2 * ROWS, FAR), BF16),
            dma((5 + CHUNKS,)),
            dma((CHUNKS, 2, HALF)),
            dma((CHUNKS, 2, HALF)),
            dma((CHUNKS, NX - 1)),
            dma((CHUNKS, NX - 1)),
            dma((CHUNKS, NMP - 1)),
            dma((CHUNKS, NMP)),
            dma((HALF, NX - 1)),
            dma((HALF, NX - 1)),
            dma((2, HALF)),
            dma((2, HALF)),
        ],
        compiler_params=pltpu.CompilerParams(
            collective_id=0, has_side_effects=True, vmem_limit_bytes=48 * 2**20
        ),
        cost_estimate=pl.CostEstimate(flops=3 * 10**9, bytes_accessed=4 * 10**6, transcendentals=0),
    )(*args)
    return pl.pallas_call(
        write,
        out_shape=tuple(jax.ShapeDtypeStruct(*shape) for shape in shapes),
        in_specs=[vmem] * 4,
        out_specs=(hbm,) * 4,
        scratch_shapes=[dma((4,))],
    )(*[pltpu.with_memory_space_constraint(r, pltpu.VMEM) for r in results])


def solution(mesh):
    return jax.shard_map(
        local,
        mesh=mesh,
        in_specs=(P("dp", None),) + (P("dp", "mp"),) * 5,
        out_specs=(P("dp", None),) + (P("dp", "mp"),) * 3,
        check_vma=False,
    )
```

```python
import functools
import math

import jax
import jax.numpy as jnp
from jax import lax
from jax.experimental import pallas as pl
from jax.experimental.pallas import tpu as pltpu
from jax.sharding import PartitionSpec as P

BIAS_ONE = 0.9999734386011124
BIAS_TWO = 0.994079470779666
NX, NZ, NMP = 4, 16, 8
ROWS = 8
GROUP = NX * ROWS
COLS = 3072
BLOCKS = COLS // 128
WIDE = 2048
FAR = WIDE // 2
NEAR = 2
W = (COLS - WIDE) // NEAR
TILE = 256
HALF = NZ // 2
NEAR_FRESH, FAR_FRESH = (1, 7), (1, 3, 5, 7)
UNIT = 2.0**20
ROOT = 1.0 / math.sqrt(128.0)
F32, BF16 = jnp.float32, jnp.bfloat16


def encode(x):
    return ((x * jnp.abs(x)) * (x * x)).astype(BF16)


def decode(y):
    y = y.astype(F32)
    size = jnp.maximum(jnp.abs(y), 2.0**-124)
    r = lax.rsqrt(size)
    return y * (r * lax.rsqrt(size * r))


def reach(fresh, s):
    return 1 if s in fresh or s + 1 not in fresh else 2


def sources(fresh, s):
    if s in fresh or s == 0:
        return []
    return [s - 1, s - 2] if s - 1 in fresh else [s - 1]


def split(x, parts):
    out = []
    for _ in range(parts):
        piece = x.astype(BF16)
        out.append(piece)
        x = x - piece.astype(F32)
    return out


def signs(size):
    i = lax.broadcasted_iota(jnp.int32, (size, size), 0)
    j = lax.broadcasted_iota(jnp.int32, (size, size), 1)
    both = i & j
    odd = both & 1
    for bit in range(1, 7):
        odd = odd ^ ((both >> bit) & 1)
    same = (i >> 7) == (j >> 7)
    return jnp.where(same, (1 - 2 * odd).astype(F32), 0.0).astype(BF16)


def dot(a, b):
    return lax.dot_general(a, b, (((1,), (0,)), ((), ())), preferred_element_type=F32)


def kernel(
    act_hbm, cot_hbm, scale_hbm, master_hbm, one_hbm, two_hbm,
    weight_out, master_out, one_out, two_out,
    act_ref, cot_ref, scale_ref, master_ref, one_ref, two_ref,
    act_t, scale_t, table, turned, values, ring_out, ring_in, x_out, x_in, w_out, w_in,
    far_out, far_in, far_values, far_ring_out, far_ring_in,
    load_sem, ring_ss, ring_rs, x_ss, x_rs, w_ss, w_rs,
    far_ss, far_rs, far_ring_ss, far_ring_rs,
):
    dp, mp = lax.axis_index("dp"), lax.axis_index("mp")
    x, z = dp // NZ, lax.rem(dp, NZ)

    def at_z(step):
        return {"dp": x * NZ + lax.rem(z + step + NZ, NZ)}

    def at_x(step):
        return {"dp": lax.rem(x + step + NX, NX) * NZ + z}

    def at_mp(step):
        return {"mp": lax.rem(mp + step + NMP, NMP)}

    loads = [(act_hbm, act_ref), (scale_hbm, scale_ref)]
    near = range(NEAR)
    pieces = ((0, 768), (768, WIDE), (WIDE, COLS))
    for lo, hi in pieces:
        loads.append((cot_hbm.at[:, lo:hi], cot_ref.at[:, lo:hi]))
    loads += [(one_hbm, one_ref), (two_hbm, two_ref), (master_hbm, master_ref)]
    loads = [pltpu.make_async_copy(s, d, load_sem.at[i]) for i, (s, d) in enumerate(loads)]
    for load in loads:
        load.start()

    barrier = pltpu.get_barrier_semaphore()
    partners = [at_z(j) for j in (1, -1, 2, -2)]
    partners += [at_x(j) for j in range(1, NX)] + [at_mp(j) for j in range(1, NMP)]
    for partner in partners:
        pl.semaphore_signal(barrier, inc=1, device_id=partner)

    table[...] = signs(TILE)
    loads[0].wait()
    act = act_ref[...].astype(F32).T
    for zd in range(NZ):
        rows = [act[(xd * NZ + zd) * ROWS : (xd * NZ + zd + 1) * ROWS] for xd in range(NX)]
        rows = jnp.concatenate(rows, axis=0).astype(BF16)
        act_t[zd * GROUP : (zd + 1) * GROUP, :] = jnp.concatenate([rows, rows], axis=1)
    loads[1].wait()
    scale = scale_ref[...].astype(F32)
    pad = jnp.ones((128 - BLOCKS, NX * NZ * ROWS), F32)
    scale = jnp.concatenate([scale, pad], axis=0).T
    for zd in range(NZ):
        for xd in range(NX):
            at = (xd * NZ + zd) * ROWS
            scale_t[zd * GROUP + xd * ROWS : zd * GROUP + (xd + 1) * ROWS, :] = scale[at : at + ROWS]
    def turn(piece):
        loads[2 + piece].wait()
        for lo in range(*pieces[piece], TILE):
            high, low = split(dot(cot_ref[:, lo : lo + TILE], table[...]), 2)
            turned[:256, lo : lo + TILE] = high
            turned[256:, lo : lo + TILE] = low

    def target(d, s):
        return lax.rem(z + (1 - 2 * d) * (HALF - s) + NZ, NZ)

    def pair(s):
        return (target(0, 0), z) if isinstance(s, int) and s == 0 else (target(0, s), target(1, s))

    def local_rows(s, begin=0, end=COLS):
        targets = pair(s)
        spans = [pl.ds(pl.multiple_of(zd * GROUP, GROUP), GROUP) for zd in targets]
        rows = jnp.concatenate([act_t[span, :] for span in spans], axis=0)
        scales = jnp.concatenate([scale_t[span, :] for span in spans], axis=0)
        inverse = ROOT / scales
        for lo in range(begin, end, TILE):
            grad = dot(rows, turned[:, lo : lo + TILE])
            for at in range(lo, lo + TILE, 128):
                b = at // 128
                scaled = grad[:, at - lo : at - lo + 128] * inverse[:, b : b + 1]
                quant = jnp.clip(scaled, -448.0, 448.0).astype(BF16).astype(F32)
                value = quant * (scales[:, b : b + 1] * UNIT)
                for i, zd in enumerate(targets):
                    values[zd, :, at : at + 128] = value[i * GROUP : (i + 1) * GROUP]
                if at < WIDE:
                    for xd in range(NX):
                        mine = [value[i * GROUP + xd * ROWS :][:ROWS] for i in range(2)]
                        far_out[s, xd, :, at : at + 128] = encode(jnp.concatenate(mine, axis=0))


    def far_copy(s, j):
        return pltpu.make_async_remote_copy(
            src_ref=far_out.at[s, lax.rem(x + j, NX)],
            dst_ref=far_in.at[s, j - 1],
            send_sem=far_ss.at[s, j - 1],
            recv_sem=far_rs.at[s, j - 1],
            device_id=at_x(j),
        )

    def far_send(s):
        for j in (2, 1, 3):
            far_copy(s, j).start()

    def far_sum(s):
        span = pl.ds(pl.multiple_of(x * ROWS, ROWS), ROWS)
        targets = pair(s)
        for j in range(1, NX):
            far_copy(s, j).wait_recv()
        for lo in range(0, WIDE, 128):
            cols = slice(lo, lo + 128)
            total = jnp.concatenate([values[zd, span, cols] for zd in targets], axis=0)
            for j in range(NX - 1):
                total = total + decode(far_in[s, j, :, cols])
            for i, zd in enumerate(targets):
                far_values[zd, :, cols] = total[i * ROWS : (i + 1) * ROWS]

    def far_ring_copy(d, s):
        return pltpu.make_async_remote_copy(
            src_ref=far_ring_out.at[d, s],
            dst_ref=far_ring_in.at[d, s],
            send_sem=far_ring_ss.at[d, s],
            recv_sem=far_ring_rs.at[d, s],
            device_id=at_z((1 - 2 * d) * reach(FAR_FRESH, s)),
        )

    def far_own(zd, lo):
        halves = [far_values[zd, :, at : at + 128] for at in (lo, FAR + lo)]
        return jnp.concatenate(halves, axis=0)

    def far_pass_on(d, s):
        zd = target(d, s)
        arrived = [t for t in sources(FAR_FRESH, s) if t or not d]
        for t in arrived:
            far_ring_copy(d, t).wait_recv()
        for lo in range(0, FAR, 128):
            total = far_own(zd, lo)
            for t in arrived:
                total = total + decode(far_ring_in[d, t, :, lo : lo + 128])
            far_ring_out[d, s, :, lo : lo + 128] = encode(total)
        far_ring_copy(d, s).start()


    def ring_copy(c, d, s, width=W):
        return pltpu.make_async_remote_copy(
            src_ref=ring_out.at[c, d, s, :, pl.ds(0, width)],
            dst_ref=ring_in.at[c, d, s, :, pl.ds(0, width)],
            send_sem=ring_ss.at[c, d, s],
            recv_sem=ring_rs.at[c, d, s],
            device_id=at_z((1 - 2 * d) * reach(NEAR_FRESH, s)),
        )

    def own(c, zd, lo):
        return values[zd, :, WIDE + c * W + lo : WIDE + c * W + lo + 128]

    def share(c, d):
        middle = (W // 256 + c % 2) * 128
        return (0, middle) if d == 0 else (middle, W)

    def width(c, d, s):
        begin, end = (0, W) if s else share(c, d)
        return end - begin

    def first(c):
        zd = target(0, 0)
        for d in range(2):
            begin, end = share(c, d)
            for lo in range(begin, end, 128):
                ring_out[c, d, 0, :, lo - begin : lo - begin + 128] = encode(own(c, zd, lo))
            ring_copy(c, d, 0, end - begin).start()

    def arrivals(c, d, s, lo):
        for t in sources(NEAR_FRESH, s):
            begin, end = (0, W) if t else share(c, d)
            if begin <= lo < end:
                yield decode(ring_in[c, d, t, :, lo - begin : lo - begin + 128])

    def await_arrivals(c, d, s):
        for t in sources(NEAR_FRESH, s):
            ring_copy(c, d, t, width(c, d, t)).wait_recv()

    def pass_on(c, d, s):
        zd = target(d, s)
        await_arrivals(c, d, s)
        for lo in range(0, W, 128):
            total = own(c, zd, lo)
            for term in arrivals(c, d, s, lo):
                total = total + term
            ring_out[c, d, s, :, lo : lo + 128] = encode(total)
        ring_copy(c, d, s).start()

    def x_copy(c, j):
        return pltpu.make_async_remote_copy(
            src_ref=x_out.at[c, lax.rem(x + j, NX)],
            dst_ref=x_in.at[c, j - 1],
            send_sem=x_ss.at[c, j - 1],
            recv_sem=x_rs.at[c, j - 1],
            device_id=at_x(j),
        )

    def w_copy(lanes, j, slot):
        return pltpu.make_async_remote_copy(
            src_ref=w_out.at[:, lanes],
            dst_ref=w_in.at[slot, :, lanes],
            send_sem=w_ss.at[min(lanes.start, 1), j - 1],
            recv_sem=w_rs.at[min(lanes.start, 1), slot],
            device_id=at_mp(j),
        )

    near_lanes, far_lanes = pl.ds(FAR, COLS // 2 - FAR), pl.ds(0, FAR)

    def update(begin, totals, lanes):
        count = len(totals)
        pieces = split(jnp.concatenate(totals, axis=0), 3)
        back = dot(pieces[0], table[:128, :128])
        back = back + dot(pieces[1], table[:128, :128])
        back = (back + dot(pieces[2], table[:128, :128])) * (ROOT / UNIT)
        blocks = []
        for b in range(count):
            cols = slice(begin + b * 128, begin + (b + 1) * 128)
            gradient = back[b * ROWS : (b + 1) * ROWS, :]
            one = 0.9 * one_ref[:, cols] + 0.1 * gradient
            two = 0.95 * two_ref[:, cols] + 0.05 * gradient * gradient
            master = master_ref[:, cols]
            change = (one / BIAS_ONE) / (jnp.sqrt(two / BIAS_TWO) + 1e-08)
            master = master - 0.01 * (change + 0.1 * master)
            one_out[:, cols] = one
            two_out[:, cols] = two
            master_out[:, cols] = master
            blocks.append(master)
        for b in range(count // 2):
            both = jnp.concatenate([blocks[b], blocks[b + count // 2]], axis=0).astype(BF16)
            at = begin // 2 + b * 128
            w_out[:, at : at + 128] = both
            w_in[mp, :, at : at + 128] = both
        for j in range(1, NMP):
            w_copy(lanes, j, mp).start()

    def gathered(begin, end, lanes):
        for j in range(1, NMP):
            w_copy(lanes, j, lax.rem(mp - j + NMP, NMP)).wait_recv()
        half = (end - begin) // 2
        for source in range(NMP):
            both = w_in[source, :, begin // 2 : end // 2].astype(F32)
            at = source * COLS + begin
            weight_out[:, at : at + half] = both[:ROWS].astype(BF16)
            weight_out[:, at + half : at + 2 * half] = both[ROWS:].astype(BF16)

    def far_step(s):
        far_sum(s)
        for d in range(2):
            if s or not d:
                far_pass_on(d, s)

    def near_step(s):
        for c in near:
            for d in range(2):
                pass_on(c, d, s)

    def rows_of(s):
        local_rows(s)
        far_send(s)

    turn(0)
    turn(1)
    local_rows(0, 0, WIDE)
    pl.semaphore_wait(barrier, len(partners))
    far_send(0)
    turn(2)
    local_rows(0, WIDE, COLS)
    for c in near:
        first(c)
    for s in (1, 2, 3):
        rows_of(s)
        if s == 1:
            near_step(1)
    for load in loads[-3:]:
        load.wait()

    near_step(2)
    far_step(0)
    rows_of(4)
    near_step(3)
    far_step(1)
    rows_of(5)
    near_step(4)
    far_step(2)
    rows_of(6)
    near_step(5)
    far_step(3)
    rows_of(7)
    near_step(7)
    near_step(6)
    far_step(4)
    far_step(5)

    for c in near:
        for d in range(2):
            await_arrivals(c, d, HALF)
        for lo in range(0, W, 128):
            total = own(c, z, lo)
            for d in range(2):
                for term in arrivals(c, d, HALF, lo):
                    total = total + term
            x_out[c, :, :, lo : lo + 128] = total.reshape(NX, ROWS, 128)
        for j in (2, 1, 3):
            x_copy(c, j).start()
    far_step(6)
    far_step(7)

    totals = []
    for c in near:
        for j in range(1, NX):
            x_copy(c, j).wait_recv()
        total = x_out[c, x]
        for j in range(1, NX):
            total = total + x_in[c, j - 1]
        totals += [total[:, lo : lo + 128] for lo in range(0, W, 128)]
    update(WIDE, totals, near_lanes)

    totals = []
    for d in range(2):
        for t in sources(FAR_FRESH, HALF):
            far_ring_copy(d, t).wait_recv()
    for lo in range(0, FAR, 128):
        total = far_own(z, lo)
        for d in range(2):
            for t in sources(FAR_FRESH, HALF):
                total = total + decode(far_ring_in[d, t, :, lo : lo + 128])
        totals.append(total)
    update(0, [t[:ROWS] for t in totals] + [t[ROWS:] for t in totals], far_lanes)

    gathered(WIDE, COLS, near_lanes)
    gathered(0, WIDE, far_lanes)

    for j in range(1, NX):
        lax.fori_loop(0, HALF, lambda s, _: (far_copy(s, j).wait_send(), 0)[1], 0)
    for d in range(2):
        for s in range(d, HALF):
            far_ring_copy(d, s).wait_send()
    for c in near:
        for d in range(2):
            for s in range(HALF):
                ring_copy(c, d, s, width(c, d, s)).wait_send()
        for j in range(1, NX):
            x_copy(c, j).wait_send()
    for j in range(1, NMP):
        w_copy(near_lanes, j, mp).wait_send()
        w_copy(far_lanes, j, mp).wait_send()


def write(*refs):
    sources, outs, sem = refs[:4], refs[4:8], refs[8]
    copies = [pltpu.make_async_copy(s, o, sem.at[i]) for i, (s, o) in enumerate(zip(sources, outs))]
    for copy in copies:
        copy.start()
    for copy in copies:
        copy.wait()


def local(activations, cotangent, block_scale, master_weight, moment_one, moment_two):
    vmem, hbm = pl.BlockSpec(memory_space=pltpu.VMEM), pl.BlockSpec(memory_space=pltpu.HBM)
    rows = NX * NZ * ROWS
    dma = pltpu.SemaphoreType.DMA
    args = (activations, cotangent, block_scale.T, master_weight, moment_one, moment_two)
    args = [pltpu.with_memory_space_constraint(arg, pltpu.HBM) for arg in args]
    shapes = (((ROWS, COLS * NMP), BF16),) + (((ROWS, COLS), F32),) * 3
    results = pl.pallas_call(
        kernel,
        out_shape=tuple(pltpu.VMEM(*shape) for shape in shapes),
        in_specs=[hbm] * 6,
        out_specs=(vmem,) * 4,
        scratch_shapes=[
            pltpu.VMEM((256, rows), BF16),
            pltpu.VMEM((256, COLS), BF16),
            pltpu.VMEM((BLOCKS, rows), BF16),
            pltpu.VMEM((ROWS, COLS), F32),
            pltpu.VMEM((ROWS, COLS), F32),
            pltpu.VMEM((ROWS, COLS), F32),
            pltpu.VMEM((rows, 512), BF16),
            pltpu.VMEM((rows, 128), F32),
            pltpu.VMEM((TILE, TILE), BF16),
            pltpu.VMEM((512, COLS), BF16),
            pltpu.VMEM((NZ, GROUP, COLS), F32),
            pltpu.VMEM((NEAR, 2, HALF, GROUP, W), BF16),
            pltpu.VMEM((NEAR, 2, HALF, GROUP, W), BF16),
            pltpu.VMEM((NEAR, NX, ROWS, W), F32),
            pltpu.VMEM((NEAR, NX - 1, ROWS, W), F32),
            pltpu.VMEM((2 * ROWS, COLS // 2), BF16),
            pltpu.VMEM((NMP, 2 * ROWS, COLS // 2), BF16),
            pltpu.VMEM((HALF, NX, 2 * ROWS, WIDE), BF16),
            pltpu.VMEM((HALF, NX - 1, 2 * ROWS, WIDE), BF16),
            pltpu.VMEM((NZ, ROWS, WIDE), F32),
            pltpu.VMEM((2, HALF, 2 * ROWS, FAR), BF16),
            pltpu.VMEM((2, HALF, 2 * ROWS, FAR), BF16),
            dma((8,)),
            dma((NEAR, 2, HALF)),
            dma((NEAR, 2, HALF)),
            dma((NEAR, NX - 1)),
            dma((NEAR, NX - 1)),
            dma((2, NMP - 1)),
            dma((2, NMP)),
            dma((HALF, NX - 1)),
            dma((HALF, NX - 1)),
            dma((2, HALF)),
            dma((2, HALF)),
        ],
        compiler_params=pltpu.CompilerParams(
            collective_id=0, has_side_effects=True, vmem_limit_bytes=48 * 2**20
        ),
        cost_estimate=pl.CostEstimate(flops=3 * 10**9, bytes_accessed=4 * 10**6, transcendentals=0),
    )(*args)
    return pl.pallas_call(
        write,
        out_shape=tuple(jax.ShapeDtypeStruct(*shape) for shape in shapes),
        in_specs=[vmem] * 4,
        out_specs=(hbm,) * 4,
        scratch_shapes=[dma((4,))],
    )(*[pltpu.with_memory_space_constraint(r, pltpu.VMEM) for r in results])


def solution(mesh):
    return jax.shard_map(
        local,
        mesh=mesh,
        in_specs=(P("dp", None),) + (P("dp", "mp"),) * 5,
        out_specs=(P("dp", None),) + (P("dp", "mp"),) * 3,
        check_vma=False,
    )
```

```python
import functools
import math

import jax
import jax.numpy as jnp
from jax import lax
from jax.experimental import pallas as pl
from jax.experimental.pallas import tpu as pltpu
from jax.sharding import PartitionSpec as P

BIAS_ONE = 0.9999734386011124
BIAS_TWO = 0.994079470779666
NX, NZ, NMP = 4, 16, 8
ROWS = 8
GROUP = NX * ROWS
COLS = 3072
BLOCKS = COLS // 128
WIDE = 2048
FAR = WIDE // 2
NEAR = 2
W = (COLS - WIDE) // NEAR
TILE = 256
HALF = NZ // 2
NEAR_FRESH, FAR_FRESH = (1, 7), (1, 3, 5, 7)
UNIT = 2.0**20
ROOT = 1.0 / math.sqrt(128.0)
F32, BF16 = jnp.float32, jnp.bfloat16


def encode(x):
    return ((x * jnp.abs(x)) * (x * x)).astype(BF16)


def decode(y):
    y = y.astype(F32)
    size = jnp.maximum(jnp.abs(y), 2.0**-124)
    r = lax.rsqrt(size)
    return y * (r * lax.rsqrt(size * r))


def reach(fresh, s):
    return 1 if s in fresh or s + 1 not in fresh else 2


def sources(fresh, s):
    if s in fresh or s == 0:
        return []
    return [s - 1, s - 2] if s - 1 in fresh else [s - 1]


def split(x, parts):
    out = []
    for _ in range(parts):
        piece = x.astype(BF16)
        out.append(piece)
        x = x - piece.astype(F32)
    return out


def signs(size):
    i = lax.broadcasted_iota(jnp.int32, (size, size), 0)
    j = lax.broadcasted_iota(jnp.int32, (size, size), 1)
    both = i & j
    odd = both & 1
    for bit in range(1, 7):
        odd = odd ^ ((both >> bit) & 1)
    same = (i >> 7) == (j >> 7)
    return jnp.where(same, (1 - 2 * odd).astype(F32), 0.0).astype(BF16)


def dot(a, b):
    return lax.dot_general(a, b, (((1,), (0,)), ((), ())), preferred_element_type=F32)


def kernel(
    act_hbm, cot_hbm, scale_hbm, master_hbm, one_hbm, two_hbm,
    weight_out, master_out, one_out, two_out,
    act_ref, cot_ref, scale_ref, master_ref, one_ref, two_ref,
    act_t, scale_t, table, turned, values, ring_out, ring_in, x_out, x_in, w_out, w_in,
    far_out, far_in, far_values, far_ring_out, far_ring_in,
    load_sem, ring_ss, ring_rs, x_ss, x_rs, w_ss, w_rs,
    far_ss, far_rs, far_ring_ss, far_ring_rs,
):
    dp, mp = lax.axis_index("dp"), lax.axis_index("mp")
    x, z = dp // NZ, lax.rem(dp, NZ)

    def at_z(step):
        return {"dp": x * NZ + lax.rem(z + step + NZ, NZ)}

    def at_x(step):
        return {"dp": lax.rem(x + step + NX, NX) * NZ + z}

    def at_mp(step):
        return {"mp": lax.rem(mp + step + NMP, NMP)}

    loads = [(act_hbm, act_ref), (scale_hbm, scale_ref)]
    near = range(NEAR)
    pieces = ((0, 768), (768, WIDE), (WIDE, COLS))
    for lo, hi in pieces:
        loads.append((cot_hbm.at[:, lo:hi], cot_ref.at[:, lo:hi]))
    loads += [(one_hbm, one_ref), (two_hbm, two_ref), (master_hbm, master_ref)]
    loads = [pltpu.make_async_copy(s, d, load_sem.at[i]) for i, (s, d) in enumerate(loads)]
    for load in loads:
        load.start()

    barrier = pltpu.get_barrier_semaphore()
    partners = [at_z(j) for j in (1, -1, 2, -2)]
    partners += [at_x(j) for j in range(1, NX)] + [at_mp(j) for j in range(1, NMP)]
    for partner in partners:
        pl.semaphore_signal(barrier, inc=1, device_id=partner)

    table[...] = signs(TILE)
    loads[0].wait()
    act = act_ref[...].astype(F32).T
    for zd in range(NZ):
        rows = [act[(xd * NZ + zd) * ROWS : (xd * NZ + zd + 1) * ROWS] for xd in range(NX)]
        rows = jnp.concatenate(rows, axis=0).astype(BF16)
        act_t[zd * GROUP : (zd + 1) * GROUP, :] = jnp.concatenate([rows, rows], axis=1)
    loads[1].wait()
    scale = scale_ref[...].astype(F32)
    pad = jnp.ones((128 - BLOCKS, NX * NZ * ROWS), F32)
    scale = jnp.concatenate([scale, pad], axis=0).T
    for zd in range(NZ):
        for xd in range(NX):
            at = (xd * NZ + zd) * ROWS
            scale_t[zd * GROUP + xd * ROWS : zd * GROUP + (xd + 1) * ROWS, :] = scale[at : at + ROWS]
    def turn(piece):
        loads[2 + piece].wait()
        for lo in range(*pieces[piece], TILE):
            high, low = split(dot(cot_ref[:, lo : lo + TILE], table[...]), 2)
            turned[:256, lo : lo + TILE] = high
            turned[256:, lo : lo + TILE] = low

    def target(d, s):
        return lax.rem(z + (1 - 2 * d) * (HALF - s) + NZ, NZ)

    def pair(s):
        return (target(0, 0), z) if isinstance(s, int) and s == 0 else (target(0, s), target(1, s))

    def local_rows(s, begin=0, end=COLS):
        targets = pair(s)
        spans = [pl.ds(pl.multiple_of(zd * GROUP, GROUP), GROUP) for zd in targets]
        rows = jnp.concatenate([act_t[span, :] for span in spans], axis=0)
        scales = jnp.concatenate([scale_t[span, :] for span in spans], axis=0)
        inverse = ROOT / scales
        for lo in range(begin, end, TILE):
            grad = dot(rows, turned[:, lo : lo + TILE])
            for at in range(lo, lo + TILE, 128):
                b = at // 128
                scaled = grad[:, at - lo : at - lo + 128] * inverse[:, b : b + 1]
                quant = jnp.clip(scaled, -448.0, 448.0).astype(BF16).astype(F32)
                value = quant * (scales[:, b : b + 1] * UNIT)
                for i, zd in enumerate(targets):
                    values[zd, :, at : at + 128] = value[i * GROUP : (i + 1) * GROUP]
                if at < WIDE:
                    for xd in range(NX):
                        mine = [value[i * GROUP + xd * ROWS :][:ROWS] for i in range(2)]
                        far_out[s, xd, :, at : at + 128] = encode(jnp.concatenate(mine, axis=0))


    def far_copy(s, j):
        return pltpu.make_async_remote_copy(
            src_ref=far_out.at[s, lax.rem(x + j, NX)],
            dst_ref=far_in.at[s, j - 1],
            send_sem=far_ss.at[s, j - 1],
            recv_sem=far_rs.at[s, j - 1],
            device_id=at_x(j),
        )

    def far_send(s):
        for j in (2, 1, 3):
            far_copy(s, j).start()

    def far_sum(s):
        span = pl.ds(pl.multiple_of(x * ROWS, ROWS), ROWS)
        targets = pair(s)
        for j in range(1, NX):
            far_copy(s, j).wait_recv()
        for lo in range(0, WIDE, 128):
            cols = slice(lo, lo + 128)
            total = jnp.concatenate([values[zd, span, cols] for zd in targets], axis=0)
            for j in range(NX - 1):
                total = total + decode(far_in[s, j, :, cols])
            for i, zd in enumerate(targets):
                far_values[zd, :, cols] = total[i * ROWS : (i + 1) * ROWS]

    def far_ring_copy(d, s):
        return pltpu.make_async_remote_copy(
            src_ref=far_ring_out.at[d, s],
            dst_ref=far_ring_in.at[d, s],
            send_sem=far_ring_ss.at[d, s],
            recv_sem=far_ring_rs.at[d, s],
            device_id=at_z((1 - 2 * d) * reach(FAR_FRESH, s)),
        )

    def far_own(zd, lo):
        halves = [far_values[zd, :, at : at + 128] for at in (lo, FAR + lo)]
        return jnp.concatenate(halves, axis=0)

    def far_pass_on(d, s):
        zd = target(d, s)
        arrived = [t for t in sources(FAR_FRESH, s) if t or not d]
        for t in arrived:
            far_ring_copy(d, t).wait_recv()
        for lo in range(0, FAR, 128):
            total = far_own(zd, lo)
            for t in arrived:
                total = total + decode(far_ring_in[d, t, :, lo : lo + 128])
            far_ring_out[d, s, :, lo : lo + 128] = encode(total)
        far_ring_copy(d, s).start()


    def ring_copy(c, d, s, width=W):
        return pltpu.make_async_remote_copy(
            src_ref=ring_out.at[c, d, s, :, pl.ds(0, width)],
            dst_ref=ring_in.at[c, d, s, :, pl.ds(0, width)],
            send_sem=ring_ss.at[c, d, s],
            recv_sem=ring_rs.at[c, d, s],
            device_id=at_z((1 - 2 * d) * reach(NEAR_FRESH, s)),
        )

    def own(c, zd, lo):
        return values[zd, :, WIDE + c * W + lo : WIDE + c * W + lo + 128]

    def share(c, d):
        middle = (W // 256 + c % 2) * 128
        return (0, middle) if d == 0 else (middle, W)

    def width(c, d, s):
        begin, end = (0, W) if s else share(c, d)
        return end - begin

    def first(c):
        zd = target(0, 0)
        for d in range(2):
            begin, end = share(c, d)
            for lo in range(begin, end, 128):
                ring_out[c, d, 0, :, lo - begin : lo - begin + 128] = encode(own(c, zd, lo))
            ring_copy(c, d, 0, end - begin).start()

    def arrivals(c, d, s, lo):
        for t in sources(NEAR_FRESH, s):
            begin, end = (0, W) if t else share(c, d)
            if begin <= lo < end:
                yield decode(ring_in[c, d, t, :, lo - begin : lo - begin + 128])

    def await_arrivals(c, d, s):
        for t in sources(NEAR_FRESH, s):
            ring_copy(c, d, t, width(c, d, t)).wait_recv()

    def pass_on(c, d, s):
        zd = target(d, s)
        await_arrivals(c, d, s)
        for lo in range(0, W, 128):
            total = own(c, zd, lo)
            for term in arrivals(c, d, s, lo):
                total = total + term
            ring_out[c, d, s, :, lo : lo + 128] = encode(total)
        ring_copy(c, d, s).start()

    def x_copy(c, j):
        return pltpu.make_async_remote_copy(
            src_ref=x_out.at[c, lax.rem(x + j, NX)],
            dst_ref=x_in.at[c, j - 1],
            send_sem=x_ss.at[c, j - 1],
            recv_sem=x_rs.at[c, j - 1],
            device_id=at_x(j),
        )

    def w_copy(lanes, j, slot):
        return pltpu.make_async_remote_copy(
            src_ref=w_out.at[:, lanes],
            dst_ref=w_in.at[slot, :, lanes],
            send_sem=w_ss.at[min(lanes.start, 1), j - 1],
            recv_sem=w_rs.at[min(lanes.start, 1), slot],
            device_id=at_mp(j),
        )

    near_lanes, far_lanes = pl.ds(FAR, COLS // 2 - FAR), pl.ds(0, FAR)

    def update(begin, totals, lanes):
        count = len(totals)
        pieces = split(jnp.concatenate(totals, axis=0), 3)
        back = dot(pieces[0], table[:128, :128])
        back = back + dot(pieces[1], table[:128, :128])
        back = (back + dot(pieces[2], table[:128, :128])) * (ROOT / UNIT)
        blocks = []
        for b in range(count):
            cols = slice(begin + b * 128, begin + (b + 1) * 128)
            gradient = back[b * ROWS : (b + 1) * ROWS, :]
            one = 0.9 * one_ref[:, cols] + 0.1 * gradient
            two = 0.95 * two_ref[:, cols] + 0.05 * gradient * gradient
            master = master_ref[:, cols]
            change = (one / BIAS_ONE) / (jnp.sqrt(two / BIAS_TWO) + 1e-08)
            master = master - 0.01 * (change + 0.1 * master)
            one_out[:, cols] = one
            two_out[:, cols] = two
            master_out[:, cols] = master
            blocks.append(master)
        for b in range(count // 2):
            both = jnp.concatenate([blocks[b], blocks[b + count // 2]], axis=0).astype(BF16)
            at = begin // 2 + b * 128
            w_out[:, at : at + 128] = both
            w_in[mp, :, at : at + 128] = both
        for j in (4, 3, 5, 2, 6, 1, 7):
            w_copy(lanes, j, mp).start()

    def gathered(begin, end, lanes):
        half = (end - begin) // 2
        for j in (0, 1, 7, 2, 6, 3, 5, 4):
            source = lax.rem(mp - j + NMP, NMP)
            if j:
                w_copy(lanes, j, source).wait_recv()
            both = w_in[source, :, begin // 2 : end // 2].astype(F32)
            at = pl.multiple_of(source * COLS + begin, 128)
            weight_out[:, pl.ds(at, half)] = both[:ROWS].astype(BF16)
            weight_out[:, pl.ds(at + half, half)] = both[ROWS:].astype(BF16)

    def far_step(s):
        far_sum(s)
        for d in range(2):
            if s or not d:
                far_pass_on(d, s)

    def near_step(s):
        for c in near:
            for d in range(2):
                pass_on(c, d, s)

    def rows_of(s):
        local_rows(s)
        far_send(s)

    turn(0)
    turn(1)
    local_rows(0, 0, WIDE)
    pl.semaphore_wait(barrier, len(partners))
    far_send(0)
    turn(2)
    local_rows(0, WIDE, COLS)
    for c in near:
        first(c)
    for s in (1, 2):
        rows_of(s)
        if s == 1:
            near_step(1)
    for load in loads[-3:]:
        load.wait()

    near_step(2)
    rows_of(3)
    far_step(0)
    rows_of(4)
    near_step(3)
    far_step(1)
    rows_of(5)
    near_step(4)
    far_step(2)
    rows_of(6)
    near_step(5)
    far_step(3)
    rows_of(7)
    near_step(7)
    near_step(6)
    far_step(4)
    far_step(5)

    for c in near:
        for d in range(2):
            await_arrivals(c, d, HALF)
        for lo in range(0, W, 128):
            total = own(c, z, lo)
            for d in range(2):
                for term in arrivals(c, d, HALF, lo):
                    total = total + term
            x_out[c, :, :, lo : lo + 128] = total.reshape(NX, ROWS, 128)
        for j in (2, 1, 3):
            x_copy(c, j).start()
    far_step(6)
    far_step(7)

    totals = []
    for c in near:
        for j in range(1, NX):
            x_copy(c, j).wait_recv()
        total = x_out[c, x]
        for j in range(1, NX):
            total = total + x_in[c, j - 1]
        totals += [total[:, lo : lo + 128] for lo in range(0, W, 128)]
    update(WIDE, totals, near_lanes)

    totals = []
    for d in range(2):
        for t in sources(FAR_FRESH, HALF):
            far_ring_copy(d, t).wait_recv()
    for lo in range(0, FAR, 128):
        total = far_own(z, lo)
        for d in range(2):
            for t in sources(FAR_FRESH, HALF):
                total = total + decode(far_ring_in[d, t, :, lo : lo + 128])
        totals.append(total)
    update(0, [t[:ROWS] for t in totals] + [t[ROWS:] for t in totals], far_lanes)

    for j in range(1, NX):
        lax.fori_loop(0, HALF, lambda s, _: (far_copy(s, j).wait_send(), 0)[1], 0)
    for d in range(2):
        for s in range(d, HALF):
            far_ring_copy(d, s).wait_send()
    for c in near:
        for d in range(2):
            for s in range(HALF):
                ring_copy(c, d, s, width(c, d, s)).wait_send()
        for j in range(1, NX):
            x_copy(c, j).wait_send()
    gathered(WIDE, COLS, near_lanes)
    gathered(0, WIDE, far_lanes)

    for j in range(1, NMP):
        w_copy(near_lanes, j, mp).wait_send()
        w_copy(far_lanes, j, mp).wait_send()


def write(*refs):
    sources, outs, sem = refs[:4], refs[4:8], refs[8]
    copies = [pltpu.make_async_copy(s, o, sem.at[i]) for i, (s, o) in enumerate(zip(sources, outs))]
    for copy in copies:
        copy.start()
    for copy in copies:
        copy.wait()


def local(activations, cotangent, block_scale, master_weight, moment_one, moment_two):
    vmem, hbm = pl.BlockSpec(memory_space=pltpu.VMEM), pl.BlockSpec(memory_space=pltpu.HBM)
    rows = NX * NZ * ROWS
    dma = pltpu.SemaphoreType.DMA
    args = (activations, cotangent, block_scale.T, master_weight, moment_one, moment_two)
    args = [pltpu.with_memory_space_constraint(arg, pltpu.HBM) for arg in args]
    shapes = (((ROWS, COLS * NMP), BF16),) + (((ROWS, COLS), F32),) * 3
    results = pl.pallas_call(
        kernel,
        out_shape=tuple(pltpu.VMEM(*shape) for shape in shapes),
        in_specs=[hbm] * 6,
        out_specs=(vmem,) * 4,
        scratch_shapes=[
            pltpu.VMEM((256, rows), BF16),
            pltpu.VMEM((256, COLS), BF16),
            pltpu.VMEM((BLOCKS, rows), BF16),
            pltpu.VMEM((ROWS, COLS), F32),
            pltpu.VMEM((ROWS, COLS), F32),
            pltpu.VMEM((ROWS, COLS), F32),
            pltpu.VMEM((rows, 512), BF16),
            pltpu.VMEM((rows, 128), F32),
            pltpu.VMEM((TILE, TILE), BF16),
            pltpu.VMEM((512, COLS), BF16),
            pltpu.VMEM((NZ, GROUP, COLS), F32),
            pltpu.VMEM((NEAR, 2, HALF, GROUP, W), BF16),
            pltpu.VMEM((NEAR, 2, HALF, GROUP, W), BF16),
            pltpu.VMEM((NEAR, NX, ROWS, W), F32),
            pltpu.VMEM((NEAR, NX - 1, ROWS, W), F32),
            pltpu.VMEM((2 * ROWS, COLS // 2), BF16),
            pltpu.VMEM((NMP, 2 * ROWS, COLS // 2), BF16),
            pltpu.VMEM((HALF, NX, 2 * ROWS, WIDE), BF16),
            pltpu.VMEM((HALF, NX - 1, 2 * ROWS, WIDE), BF16),
            pltpu.VMEM((NZ, ROWS, WIDE), F32),
            pltpu.VMEM((2, HALF, 2 * ROWS, FAR), BF16),
            pltpu.VMEM((2, HALF, 2 * ROWS, FAR), BF16),
            dma((8,)),
            dma((NEAR, 2, HALF)),
            dma((NEAR, 2, HALF)),
            dma((NEAR, NX - 1)),
            dma((NEAR, NX - 1)),
            dma((2, NMP - 1)),
            dma((2, NMP)),
            dma((HALF, NX - 1)),
            dma((HALF, NX - 1)),
            dma((2, HALF)),
            dma((2, HALF)),
        ],
        compiler_params=pltpu.CompilerParams(
            collective_id=0, has_side_effects=True, vmem_limit_bytes=48 * 2**20
        ),
        cost_estimate=pl.CostEstimate(flops=3 * 10**9, bytes_accessed=4 * 10**6, transcendentals=0),
    )(*args)
    return pl.pallas_call(
        write,
        out_shape=tuple(jax.ShapeDtypeStruct(*shape) for shape in shapes),
        in_specs=[vmem] * 4,
        out_specs=(hbm,) * 4,
        scratch_shapes=[dma((4,))],
    )(*[pltpu.with_memory_space_constraint(r, pltpu.VMEM) for r in results])


def solution(mesh):
    return jax.shard_map(
        local,
        mesh=mesh,
        in_specs=(P("dp", None),) + (P("dp", "mp"),) * 5,
        out_specs=(P("dp", None),) + (P("dp", "mp"),) * 3,
        check_vma=False,
    )
```

```python
import functools
import math

import jax
import jax.numpy as jnp
from jax import lax
from jax.experimental import pallas as pl
from jax.experimental.pallas import tpu as pltpu
from jax.sharding import PartitionSpec as P

BIAS_ONE = 0.9999734386011124
BIAS_TWO = 0.994079470779666
NX, NZ, NMP = 4, 16, 8
ROWS = 8
GROUP = NX * ROWS
COLS = 3072
BLOCKS = COLS // 128
WIDE = 2048
FAR = WIDE // 2
NEAR = 2
W = (COLS - WIDE) // NEAR
TILE = 256
HALF = NZ // 2
NEAR_FRESH, FAR_FRESH = (1, 7), (1, 3, 5, 7)
UNIT = 2.0**20
ROOT = 1.0 / math.sqrt(128.0)
F32, BF16 = jnp.float32, jnp.bfloat16


def encode(x):
    return ((x * jnp.abs(x)) * (x * x)).astype(BF16)


def decode(y):
    y = y.astype(F32)
    size = jnp.maximum(jnp.abs(y), 2.0**-124)
    r = lax.rsqrt(size)
    return y * (r * lax.rsqrt(size * r))


def reach(fresh, s):
    return 1 if s in fresh or s + 1 not in fresh else 2


def sources(fresh, s):
    if s in fresh or s == 0:
        return []
    return [s - 1, s - 2] if s - 1 in fresh else [s - 1]


def split(x, parts):
    out = []
    for _ in range(parts):
        piece = x.astype(BF16)
        out.append(piece)
        x = x - piece.astype(F32)
    return out


def signs(size):
    i = lax.broadcasted_iota(jnp.int32, (size, size), 0)
    j = lax.broadcasted_iota(jnp.int32, (size, size), 1)
    both = i & j
    odd = both & 1
    for bit in range(1, 7):
        odd = odd ^ ((both >> bit) & 1)
    same = (i >> 7) == (j >> 7)
    return jnp.where(same, (1 - 2 * odd).astype(F32), 0.0).astype(BF16)


def dot(a, b):
    return lax.dot_general(a, b, (((1,), (0,)), ((), ())), preferred_element_type=F32)


def kernel(
    act_hbm, cot_hbm, scale_hbm, master_hbm, one_hbm, two_hbm,
    weight_out, master_out, one_out, two_out,
    act_ref, cot_ref, scale_ref, master_ref, one_ref, two_ref,
    act_t, scale_t, table, turned, values, ring_out, ring_in, x_out, x_in, w_out, w_in,
    far_out, far_in, far_values, far_ring_out, far_ring_in,
    load_sem, ring_ss, ring_rs, x_ss, x_rs, w_ss, w_rs,
    far_ss, far_rs, far_ring_ss, far_ring_rs,
):
    dp, mp = lax.axis_index("dp"), lax.axis_index("mp")
    x, z = dp // NZ, lax.rem(dp, NZ)

    def at_z(step):
        return {"dp": x * NZ + lax.rem(z + step + NZ, NZ)}

    def at_x(step):
        return {"dp": lax.rem(x + step + NX, NX) * NZ + z}

    def at_mp(step):
        return {"mp": lax.rem(mp + step + NMP, NMP)}

    loads = [(act_hbm, act_ref), (scale_hbm, scale_ref)]
    near = range(NEAR)
    pieces = ((0, 768), (768, WIDE), (WIDE, COLS))
    for lo, hi in pieces:
        loads.append((cot_hbm.at[:, lo:hi], cot_ref.at[:, lo:hi]))
    loads += [(one_hbm, one_ref), (two_hbm, two_ref), (master_hbm, master_ref)]
    loads = [pltpu.make_async_copy(s, d, load_sem.at[i]) for i, (s, d) in enumerate(loads)]
    for load in loads:
        load.start()

    barrier = pltpu.get_barrier_semaphore()
    partners = [at_z(j) for j in (1, -1, 2, -2)]
    partners += [at_x(j) for j in range(1, NX)] + [at_mp(j) for j in range(1, NMP)]
    for partner in partners:
        pl.semaphore_signal(barrier, inc=1, device_id=partner)

    table[...] = signs(TILE)
    loads[0].wait()
    act = act_ref[...].astype(F32).T
    for zd in range(NZ):
        rows = [act[(xd * NZ + zd) * ROWS : (xd * NZ + zd + 1) * ROWS] for xd in range(NX)]
        rows = jnp.concatenate(rows, axis=0).astype(BF16)
        act_t[zd * GROUP : (zd + 1) * GROUP, :] = jnp.concatenate([rows, rows], axis=1)
    loads[1].wait()
    scale = scale_ref[...].astype(F32)
    pad = jnp.ones((128 - BLOCKS, NX * NZ * ROWS), F32)
    scale = jnp.concatenate([scale, pad], axis=0).T
    for zd in range(NZ):
        for xd in range(NX):
            at = (xd * NZ + zd) * ROWS
            scale_t[zd * GROUP + xd * ROWS : zd * GROUP + (xd + 1) * ROWS, :] = scale[at : at + ROWS]
    def turn(piece):
        loads[2 + piece].wait()
        for lo in range(*pieces[piece], TILE):
            high, low = split(dot(cot_ref[:, lo : lo + TILE], table[...]), 2)
            turned[:256, lo : lo + TILE] = high
            turned[256:, lo : lo + TILE] = low

    def target(d, s):
        return lax.rem(z + (1 - 2 * d) * (HALF - s) + NZ, NZ)

    def pair(s):
        return (target(0, 0), z) if isinstance(s, int) and s == 0 else (target(0, s), target(1, s))

    def local_rows(s, begin=0, end=COLS):
        targets = pair(s)
        spans = [pl.ds(pl.multiple_of(zd * GROUP, GROUP), GROUP) for zd in targets]
        rows = jnp.concatenate([act_t[span, :] for span in spans], axis=0)
        scales = jnp.concatenate([scale_t[span, :] for span in spans], axis=0)
        inverse = ROOT / scales
        for lo in range(begin, end, TILE):
            grad = dot(rows, turned[:, lo : lo + TILE])
            for at in range(lo, lo + TILE, 128):
                b = at // 128
                scaled = grad[:, at - lo : at - lo + 128] * inverse[:, b : b + 1]
                quant = jnp.clip(scaled, -448.0, 448.0).astype(BF16).astype(F32)
                value = quant * (scales[:, b : b + 1] * UNIT)
                for i, zd in enumerate(targets):
                    values[zd, :, at : at + 128] = value[i * GROUP : (i + 1) * GROUP]
                if at < WIDE:
                    for xd in range(NX):
                        mine = [value[i * GROUP + xd * ROWS :][:ROWS] for i in range(2)]
                        far_out[s, xd, :, at : at + 128] = encode(jnp.concatenate(mine, axis=0))


    def far_copy(s, j):
        return pltpu.make_async_remote_copy(
            src_ref=far_out.at[s, lax.rem(x + j, NX)],
            dst_ref=far_in.at[s, j - 1],
            send_sem=far_ss.at[s, j - 1],
            recv_sem=far_rs.at[s, j - 1],
            device_id=at_x(j),
        )

    def far_send(s):
        for j in (1, 3, 2):
            far_copy(s, j).start()

    def far_sum(s):
        span = pl.ds(pl.multiple_of(x * ROWS, ROWS), ROWS)
        targets = pair(s)
        for j in range(1, NX):
            far_copy(s, j).wait_recv()
        for lo in range(0, WIDE, 128):
            cols = slice(lo, lo + 128)
            total = jnp.concatenate([values[zd, span, cols] for zd in targets], axis=0)
            for j in range(NX - 1):
                total = total + decode(far_in[s, j, :, cols])
            for i, zd in enumerate(targets):
                far_values[zd, :, cols] = total[i * ROWS : (i + 1) * ROWS]

    def far_ring_copy(d, s):
        return pltpu.make_async_remote_copy(
            src_ref=far_ring_out.at[d, s],
            dst_ref=far_ring_in.at[d, s],
            send_sem=far_ring_ss.at[d, s],
            recv_sem=far_ring_rs.at[d, s],
            device_id=at_z((1 - 2 * d) * reach(FAR_FRESH, s)),
        )

    def far_own(zd, lo):
        halves = [far_values[zd, :, at : at + 128] for at in (lo, FAR + lo)]
        return jnp.concatenate(halves, axis=0)

    def far_pass_on(d, s):
        zd = target(d, s)
        arrived = [t for t in sources(FAR_FRESH, s) if t or not d]
        for t in arrived:
            far_ring_copy(d, t).wait_recv()
        for lo in range(0, FAR, 128):
            total = far_own(zd, lo)
            for t in arrived:
                total = total + decode(far_ring_in[d, t, :, lo : lo + 128])
            far_ring_out[d, s, :, lo : lo + 128] = encode(total)
        far_ring_copy(d, s).start()


    def ring_copy(c, d, s, width=W):
        return pltpu.make_async_remote_copy(
            src_ref=ring_out.at[c, d, s, :, pl.ds(0, width)],
            dst_ref=ring_in.at[c, d, s, :, pl.ds(0, width)],
            send_sem=ring_ss.at[c, d, s],
            recv_sem=ring_rs.at[c, d, s],
            device_id=at_z((1 - 2 * d) * reach(NEAR_FRESH, s)),
        )

    def own(c, zd, lo):
        return values[zd, :, WIDE + c * W + lo : WIDE + c * W + lo + 128]

    def share(c, d):
        middle = (W // 256 + c % 2) * 128
        return (0, middle) if d == 0 else (middle, W)

    def width(c, d, s):
        begin, end = (0, W) if s else share(c, d)
        return end - begin

    def first(c):
        zd = target(0, 0)
        for d in range(2):
            begin, end = share(c, d)
            for lo in range(begin, end, 128):
                ring_out[c, d, 0, :, lo - begin : lo - begin + 128] = encode(own(c, zd, lo))
            ring_copy(c, d, 0, end - begin).start()

    def arrivals(c, d, s, lo):
        for t in sources(NEAR_FRESH, s):
            begin, end = (0, W) if t else share(c, d)
            if begin <= lo < end:
                yield decode(ring_in[c, d, t, :, lo - begin : lo - begin + 128])

    def await_arrivals(c, d, s):
        for t in sources(NEAR_FRESH, s):
            ring_copy(c, d, t, width(c, d, t)).wait_recv()

    def pass_on(c, d, s):
        zd = target(d, s)
        await_arrivals(c, d, s)
        for lo in range(0, W, 128):
            total = own(c, zd, lo)
            for term in arrivals(c, d, s, lo):
                total = total + term
            ring_out[c, d, s, :, lo : lo + 128] = encode(total)
        ring_copy(c, d, s).start()

    def x_copy(c, j):
        return pltpu.make_async_remote_copy(
            src_ref=x_out.at[c, lax.rem(x + j, NX)],
            dst_ref=x_in.at[c, j - 1],
            send_sem=x_ss.at[c, j - 1],
            recv_sem=x_rs.at[c, j - 1],
            device_id=at_x(j),
        )

    def w_copy(lanes, j, slot):
        return pltpu.make_async_remote_copy(
            src_ref=w_out.at[:, lanes],
            dst_ref=w_in.at[slot, :, lanes],
            send_sem=w_ss.at[min(lanes.start, 1), j - 1],
            recv_sem=w_rs.at[min(lanes.start, 1), slot],
            device_id=at_mp(j),
        )

    near_lanes, far_lanes = pl.ds(FAR, COLS // 2 - FAR), pl.ds(0, FAR)

    def update(begin, totals, lanes):
        count = len(totals)
        pieces = split(jnp.concatenate(totals, axis=0), 3)
        back = dot(pieces[0], table[:128, :128])
        back = back + dot(pieces[1], table[:128, :128])
        back = (back + dot(pieces[2], table[:128, :128])) * (ROOT / UNIT)
        blocks = []
        for b in range(count):
            cols = slice(begin + b * 128, begin + (b + 1) * 128)
            gradient = back[b * ROWS : (b + 1) * ROWS, :]
            one = 0.9 * one_ref[:, cols] + 0.1 * gradient
            two = 0.95 * two_ref[:, cols] + 0.05 * gradient * gradient
            master = master_ref[:, cols]
            change = (one / BIAS_ONE) / (jnp.sqrt(two / BIAS_TWO) + 1e-08)
            master = master - 0.01 * (change + 0.1 * master)
            one_out[:, cols] = one
            two_out[:, cols] = two
            master_out[:, cols] = master
            blocks.append(master)
        for b in range(count // 2):
            both = jnp.concatenate([blocks[b], blocks[b + count // 2]], axis=0).astype(BF16)
            at = begin // 2 + b * 128
            w_out[:, at : at + 128] = both
            w_in[mp, :, at : at + 128] = both
        for j in (4, 3, 5, 2, 6, 1, 7):
            w_copy(lanes, j, mp).start()

    def gathered(begin, end, lanes):
        half = (end - begin) // 2
        for j in (0, 1, 7, 2, 6, 3, 5, 4):
            source = lax.rem(mp - j + NMP, NMP)
            if j:
                w_copy(lanes, j, source).wait_recv()
            both = w_in[source, :, begin // 2 : end // 2].astype(F32)
            at = pl.multiple_of(source * COLS + begin, 128)
            weight_out[:, pl.ds(at, half)] = both[:ROWS].astype(BF16)
            weight_out[:, pl.ds(at + half, half)] = both[ROWS:].astype(BF16)

    def far_step(s):
        far_sum(s)
        for d in range(2):
            if s or not d:
                far_pass_on(d, s)

    def near_step(s):
        for c in near:
            for d in range(2):
                pass_on(c, d, s)

    def rows_of(s):
        local_rows(s)
        far_send(s)

    turn(0)
    turn(1)
    local_rows(0, 0, WIDE)
    pl.semaphore_wait(barrier, len(partners))
    far_send(0)
    turn(2)
    local_rows(0, WIDE, COLS)
    for c in near:
        first(c)
    for s in (1, 2):
        rows_of(s)
        if s == 1:
            near_step(1)
    for load in loads[-3:]:
        load.wait()

    near_step(2)
    rows_of(3)
    far_step(0)
    rows_of(4)
    near_step(3)
    far_step(1)
    rows_of(5)
    near_step(4)
    far_step(2)
    rows_of(6)
    near_step(5)
    far_step(3)
    rows_of(7)
    near_step(7)
    near_step(6)
    far_step(4)
    far_step(5)

    for c in near:
        for d in range(2):
            await_arrivals(c, d, HALF)
        for lo in range(0, W, 128):
            total = own(c, z, lo)
            for d in range(2):
                for term in arrivals(c, d, HALF, lo):
                    total = total + term
            x_out[c, :, :, lo : lo + 128] = total.reshape(NX, ROWS, 128)
        for j in (2, 1, 3):
            x_copy(c, j).start()
    far_step(6)
    far_step(7)

    totals = []
    for c in near:
        for j in range(1, NX):
            x_copy(c, j).wait_recv()
        total = x_out[c, x]
        for j in range(1, NX):
            total = total + x_in[c, j - 1]
        totals += [total[:, lo : lo + 128] for lo in range(0, W, 128)]
    update(WIDE, totals, near_lanes)

    totals = []
    for d in range(2):
        for t in sources(FAR_FRESH, HALF):
            far_ring_copy(d, t).wait_recv()
    for lo in range(0, FAR, 128):
        total = far_own(z, lo)
        for d in range(2):
            for t in sources(FAR_FRESH, HALF):
                total = total + decode(far_ring_in[d, t, :, lo : lo + 128])
        totals.append(total)
    update(0, [t[:ROWS] for t in totals] + [t[ROWS:] for t in totals], far_lanes)

    for j in range(1, NX):
        lax.fori_loop(0, HALF, lambda s, _: (far_copy(s, j).wait_send(), 0)[1], 0)
    for d in range(2):
        for s in range(d, HALF):
            far_ring_copy(d, s).wait_send()
    for c in near:
        for d in range(2):
            for s in range(HALF):
                ring_copy(c, d, s, width(c, d, s)).wait_send()
        for j in range(1, NX):
            x_copy(c, j).wait_send()
    gathered(WIDE, COLS, near_lanes)
    gathered(0, WIDE, far_lanes)

    for j in range(1, NMP):
        w_copy(near_lanes, j, mp).wait_send()
        w_copy(far_lanes, j, mp).wait_send()


def write(*refs):
    sources, outs, sem = refs[:4], refs[4:8], refs[8]
    copies = [pltpu.make_async_copy(s, o, sem.at[i]) for i, (s, o) in enumerate(zip(sources, outs))]
    for copy in copies:
        copy.start()
    for copy in copies:
        copy.wait()


def local(activations, cotangent, block_scale, master_weight, moment_one, moment_two):
    vmem, hbm = pl.BlockSpec(memory_space=pltpu.VMEM), pl.BlockSpec(memory_space=pltpu.HBM)
    rows = NX * NZ * ROWS
    dma = pltpu.SemaphoreType.DMA
    args = (activations, cotangent, block_scale.T, master_weight, moment_one, moment_two)
    args = [pltpu.with_memory_space_constraint(arg, pltpu.HBM) for arg in args]
    shapes = (((ROWS, COLS * NMP), BF16),) + (((ROWS, COLS), F32),) * 3
    results = pl.pallas_call(
        kernel,
        out_shape=tuple(pltpu.VMEM(*shape) for shape in shapes),
        in_specs=[hbm] * 6,
        out_specs=(vmem,) * 4,
        scratch_shapes=[
            pltpu.VMEM((256, rows), BF16),
            pltpu.VMEM((256, COLS), BF16),
            pltpu.VMEM((BLOCKS, rows), BF16),
            pltpu.VMEM((ROWS, COLS), F32),
            pltpu.VMEM((ROWS, COLS), F32),
            pltpu.VMEM((ROWS, COLS), F32),
            pltpu.VMEM((rows, 512), BF16),
            pltpu.VMEM((rows, 128), F32),
            pltpu.VMEM((TILE, TILE), BF16),
            pltpu.VMEM((512, COLS), BF16),
            pltpu.VMEM((NZ, GROUP, COLS), F32),
            pltpu.VMEM((NEAR, 2, HALF, GROUP, W), BF16),
            pltpu.VMEM((NEAR, 2, HALF, GROUP, W), BF16),
            pltpu.VMEM((NEAR, NX, ROWS, W), F32),
            pltpu.VMEM((NEAR, NX - 1, ROWS, W), F32),
            pltpu.VMEM((2 * ROWS, COLS // 2), BF16),
            pltpu.VMEM((NMP, 2 * ROWS, COLS // 2), BF16),
            pltpu.VMEM((HALF, NX, 2 * ROWS, WIDE), BF16),
            pltpu.VMEM((HALF, NX - 1, 2 * ROWS, WIDE), BF16),
            pltpu.VMEM((NZ, ROWS, WIDE), F32),
            pltpu.VMEM((2, HALF, 2 * ROWS, FAR), BF16),
            pltpu.VMEM((2, HALF, 2 * ROWS, FAR), BF16),
            dma((8,)),
            dma((NEAR, 2, HALF)),
            dma((NEAR, 2, HALF)),
            dma((NEAR, NX - 1)),
            dma((NEAR, NX - 1)),
            dma((2, NMP - 1)),
            dma((2, NMP)),
            dma((HALF, NX - 1)),
            dma((HALF, NX - 1)),
            dma((2, HALF)),
            dma((2, HALF)),
        ],
        compiler_params=pltpu.CompilerParams(
            collective_id=0, has_side_effects=True, vmem_limit_bytes=48 * 2**20
        ),
        cost_estimate=pl.CostEstimate(flops=3 * 10**9, bytes_accessed=4 * 10**6, transcendentals=0),
    )(*args)
    return pl.pallas_call(
        write,
        out_shape=tuple(jax.ShapeDtypeStruct(*shape) for shape in shapes),
        in_specs=[vmem] * 4,
        out_specs=(hbm,) * 4,
        scratch_shapes=[dma((4,))],
    )(*[pltpu.with_memory_space_constraint(r, pltpu.VMEM) for r in results])


def solution(mesh):
    return jax.shard_map(
        local,
        mesh=mesh,
        in_specs=(P("dp", None),) + (P("dp", "mp"),) * 5,
        out_specs=(P("dp", None),) + (P("dp", "mp"),) * 3,
        check_vma=False,
    )
```
